32 devices in a mesh: cd: 4 (over y, x), ab: 8 (over z, core).
Axes of the slice: x: 2, y: 2, z: 4, core: 2. Of those that a mesh axis runs over, the one named last changes fastest.
Arguments:
- amplitudes: float32 [2048, 16384], P('ab', 'cd'), may hold values from -6 to 6
- amp_tiles: int32 [16, 16], P('ab', 'cd'), may hold values 0 or 1
- integrals: float32 [16384, 16384], P('cd', 'ab'), may hold values from -0.046875 to 0.046875
- int_tiles: int32 [16, 16], P('cd', 'ab'), may hold values 0 or 1
- owner_tiles: int32 [16], replicated, may hold values from 0 to 15, each once
- other_terms: float32 [2048, 16384], P('cd', 'ab'), may hold values from -6 to 6
- denominators: float32 [2048, 16384], P('cd', 'ab'), may hold values from -4 to -0.5
Outputs:
- update: float32 [2048, 16384], P('cd', 'ab')
The draws below stay inside these ranges and needn't reach their ends.
Inputs may be any that keep to these rules, and one draw needn't show every extreme that they name: owner_tiles is a permutation of the row tiles.
All inputs are finite; a program needn't handle non-finite values. No bound on the sum of `amp_tiles` or of `int_tiles` on one device may be relied on, other than what follows from the above.
Results may differ from the reference program's by a relative error of at most 0.00013.
Values sent between devices are 32-bit elements; how exact they have to be, the bound alone decides.
No kernel may reach another device: no remote copies, remote signals or barrier semaphores. Data moves between devices by JAX's collectives and lax.ppermute only.
A program may use at most 256 MiB of HBM per device.

```python
import jax
import jax.numpy as jnp
from jax import lax

PAIRS = 2048
CD = 16384
AB = 16384
TILE = 1024
TILE_ROWS = 128


def place_ends(entries, key, low, top_value):
    spot = [jax.random.randint(jax.random.fold_in(key, axis), (), 0, length) for axis, length in enumerate(entries.shape)]
    main_axis = entries.shape.index(max(entries.shape))
    beside = spot[:main_axis] + [(spot[main_axis] + 1) % entries.shape[main_axis]] + spot[main_axis + 1:]
    return entries.at[tuple(spot)].set(low).at[tuple(beside)].set(top_value)


def steps_of(rng, shape, shards, least, largest):
    loudness, own = 1.0, jax.random.fold_in(rng, 6)
    for axis_at, blocks in shards:
        heights = jnp.exp(jax.random.uniform(jax.random.fold_in(own, axis_at), (blocks,), jnp.float32, least / len(shards), largest / len(shards)))
        loudness = loudness * jnp.repeat(heights, shape[axis_at] // blocks).reshape([-1 if axis == axis_at else 1 for axis in range(len(shape))])
    return loudness


def scatter_about(own_key, dims, deviation, most, shards=(), kind=jnp.bfloat16):
    array = deviation * jax.random.normal(own_key, dims, jnp.float32)
    if shards:
        array = array * steps_of(own_key, dims, shards, -0.22, 0.18)
    return jnp.clip(array, -most, most).astype(kind)


def setup_inputs(seed: int = 0) -> dict:
    keys = jax.random.split(jax.random.key(seed), 8)
    amplitudes = scatter_about(keys[0], (PAIRS, CD), 1.0, 6.0, ((0, 8), (1, 4)), jnp.float32)
    amp_tiles = place_ends((jax.random.randint(keys[1], (PAIRS // TILE_ROWS, CD // TILE), 0, 3) < 2).astype(jnp.int32), jax.random.fold_in(keys[1], 1), 0, 1)
    integrals = scatter_about(keys[2], (CD, AB), CD ** -0.5, 0.046875, ((0, 4), (1, 8)), jnp.float32)
    int_tiles = place_ends((jax.random.randint(keys[3], (CD // TILE, AB // TILE), 0, 3) < 2).astype(jnp.int32), jax.random.fold_in(keys[3], 1), 0, 1)
    owner_tiles = jax.random.permutation(keys[4], PAIRS // TILE_ROWS).astype(jnp.int32)
    other_terms = scatter_about(keys[5], (PAIRS, AB), 1.0, 6.0, ((0, 4), (1, 8)), jnp.float32)
    denominators = jnp.clip(-4.0 + 3.5 * jax.random.uniform(keys[6], (PAIRS, AB), jnp.float32) ** steps_of(keys[6], (PAIRS, AB), ((0, 4), (1, 8)), -0.2, 0.2), -4.0, -0.5)
    return {"amplitudes": amplitudes, "amp_tiles": amp_tiles, "integrals": integrals, "int_tiles": int_tiles, "owner_tiles": owner_tiles, "other_terms": other_terms, "denominators": denominators}


def spread_tiles(tile_flags, row_span, col_span):
    tile_rows, tile_cols = tile_flags.shape
    values = tile_flags.astype(jnp.float32)
    return jnp.broadcast_to(values[:, None, :, None], (tile_rows, row_span, tile_cols, col_span)).reshape(tile_rows * row_span, tile_cols * col_span)


def reference(amplitudes, amp_tiles, integrals, int_tiles, owner_tiles, other_terms, denominators):
    masked_amps = amplitudes * spread_tiles(amp_tiles, TILE_ROWS, TILE)
    masked_ints = integrals * spread_tiles(int_tiles, TILE, TILE)
    ladder = jnp.dot(masked_amps, masked_ints, precision=lax.Precision.HIGHEST, preferred_element_type=jnp.float32)
    owned = ladder.reshape(PAIRS // TILE_ROWS, TILE_ROWS, AB)[owner_tiles].reshape(PAIRS, AB)
    return (owned + other_terms) / denominators
```

```python
import functools
import itertools

import jax
import jax.numpy as jnp
from jax import lax
from jax.experimental import pallas as pl
from jax.experimental.pallas import tpu as pltpu
from jax.sharding import PartitionSpec as P

TILE = 1024
TILE_ROWS = 128
CORES = 2
VMEM_BYTES = 58 * 1024 * 1024


def spread_tiles(tile_flags, row_span, col_span):
    tile_rows, tile_cols = tile_flags.shape
    values = tile_flags.astype(jnp.float32)
    return jnp.broadcast_to(
        values[:, None, :, None], (tile_rows, row_span, tile_cols, col_span)
    ).reshape(tile_rows * row_span, tile_cols * col_span)


def plain(amplitudes, amp_tiles, integrals, int_tiles, owner_tiles, other_terms, denominators):
    masked_ints = integrals * spread_tiles(int_tiles, TILE, TILE)
    masked_amps = amplitudes * spread_tiles(amp_tiles, TILE_ROWS, TILE)
    tile_count = owner_tiles.shape[0]
    gathered = lax.all_gather(masked_amps, "ab", axis=0, tiled=True)
    partial_value = jnp.dot(
        gathered, masked_ints, precision=lax.Precision.HIGHEST, preferred_element_type=jnp.float32
    )
    col_width = partial_value.shape[1]
    partial_value = partial_value.reshape(tile_count, TILE_ROWS, col_width)[owner_tiles].reshape(
        tile_count * TILE_ROWS, col_width
    )
    owned = lax.psum_scatter(partial_value, "cd", scatter_dimension=0, tiled=True)
    return (owned + other_terms) / denominators


def plan_kernel(chips, rounds, owner_ref, pick_ref, source_ref, slot_ref, place_ref):
    for q in range(chips * rounds):
        place_ref[owner_ref[q]] = q
    owner = [[place_ref[z * rounds + k] // rounds for k in range(rounds)] for z in range(chips)]
    left = [
        [sum((owner[z][k] == c).astype(jnp.int32) for k in range(rounds)) for c in range(chips)]
        for z in range(chips)
    ]
    used = [[jnp.int32(0)] * rounds for _ in range(chips)]
    for r in range(rounds):
        there = [[jnp.minimum(left[z][c], 1) for c in range(chips)] for z in range(chips)]
        code = jnp.int32(0)
        for order in itertools.permutations(range(chips)):
            fits = there[0][order[0]]
            for z in range(1, chips):
                fits = fits * there[z][order[z]]
            code = jnp.where(fits > 0, sum(c << (4 * z) for z, c in enumerate(order)), code)
        for z in range(chips):
            target = (code >> (4 * z)) & 15
            for c in range(chips):
                left[z][c] = left[z][c] - (target == c).astype(jnp.int32)
            pick = jnp.int32(0)
            for k in range(rounds):
                free = (owner[z][k] == target).astype(jnp.int32) * (1 - used[z][k])
                pick = jnp.where(free > 0, k, pick)
            for k in range(rounds):
                used[z][k] = jnp.maximum(used[z][k], (pick == k).astype(jnp.int32))
            pick_ref[r * chips + z] = pick
            source_ref[r * chips + target] = z
            slot_ref[r * chips + target] = place_ref[z * rounds + pick] % rounds


def plan(owner_tiles, chips, rounds):
    count = jax.ShapeDtypeStruct((chips * rounds,), jnp.int32)
    smem = pl.BlockSpec(memory_space=pltpu.SMEM)
    return pl.pallas_call(
        functools.partial(plan_kernel, chips, rounds),
        out_shape=(count, count, count),
        in_specs=[smem],
        out_specs=(smem, smem, smem),
        scratch_shapes=[pltpu.SMEM((chips * rounds,), jnp.int32)],
    )(owner_tiles)


def half_kernel(core_ref, flag_ref, amp_ref, out_ref):
    tiles = flag_ref.shape[1] // CORES
    flag = flag_ref[pl.program_id(0), (1 - core_ref[0]) * tiles + pl.program_id(1)]
    out_ref[...] = amp_ref[...] * flag.astype(jnp.float32)


def other_half(core, amp_tiles, amplitudes):
    rows, depth = amplitudes.shape
    tiles = depth // TILE // CORES
    return pl.pallas_call(
        half_kernel,
        out_shape=jax.ShapeDtypeStruct((rows, depth // CORES), jnp.float32),
        grid_spec=pltpu.PrefetchScalarGridSpec(
            num_scalar_prefetch=2,
            grid=(rows // TILE_ROWS, tiles),
            in_specs=[
                pl.BlockSpec((TILE_ROWS, TILE), lambda i, j, core, flags: (i, (1 - core[0]) * tiles + j))
            ],
            out_specs=pl.BlockSpec((TILE_ROWS, TILE), lambda i, j, core, flags: (i, j)),
        ),
    )(core, amp_tiles, amplitudes)


def pack_kernel(core_ref, pick_ref, flag_ref, amp_ref, swapped_ref, out_ref):
    tiles = flag_ref.shape[1] // CORES
    per_core = flag_ref.shape[0]
    core = core_ref[0]
    pick = pick_ref[0]
    mine = pick // per_core == core

    @pl.when(mine)
    def _():
        for j in range(tiles):
            flag = flag_ref[pick % per_core, core * tiles + j].astype(jnp.float32)
            columns = pl.ds(j * TILE, TILE)
            out_ref[:, columns] = amp_ref[:, columns] * flag

    @pl.when(jnp.logical_not(mine))
    def _():
        out_ref[...] = swapped_ref[...]


def pack(core, pick, amp_tiles, amplitudes, swapped):
    per_core = amp_tiles.shape[0]
    half = swapped.shape[1]
    return pl.pallas_call(
        pack_kernel,
        out_shape=jax.ShapeDtypeStruct((TILE_ROWS, half), jnp.float32),
        grid_spec=pltpu.PrefetchScalarGridSpec(
            num_scalar_prefetch=3,
            grid=(1,),
            in_specs=[
                pl.BlockSpec((TILE_ROWS, half), lambda i, core, pick, flags: (pick[0] % per_core, core[0])),
                pl.BlockSpec((TILE_ROWS, half), lambda i, core, pick, flags: (pick[0] % per_core, 0)),
            ],
            out_specs=pl.BlockSpec((TILE_ROWS, half), lambda i, core, pick, flags: (0, 0)),
        ),
    )(core, pick, amp_tiles, amplitudes, swapped)


def split_kernel(value_ref, high_ref, low_ref):
    value = value_ref[...]
    high = value.astype(jnp.bfloat16)
    high_ref[...] = high
    low_ref[...] = (value - high.astype(jnp.float32)).astype(jnp.bfloat16)


def split(integrals):
    depth, width = integrals.shape
    rows = TILE // 2
    block = pl.BlockSpec((rows, width), lambda i: (i, 0))
    half = jax.ShapeDtypeStruct((depth, width), jnp.bfloat16)
    return pl.pallas_call(
        split_kernel,
        out_shape=(half, half),
        grid=(depth // rows,),
        in_specs=[block],
        out_specs=(block, block),
        compiler_params=pltpu.CompilerParams(vmem_limit_bytes=VMEM_BYTES),
        cost_estimate=pl.CostEstimate(flops=0, bytes_accessed=8 * depth * width, transcendentals=0),
    )(integrals)


def product_kernel(ranks, source_ref, flag_ref, amp_ref, high_ref, low_ref, *rest):
    out_refs, (pair_ref, total_ref) = rest[:ranks], rest[ranks:]
    rows = ranks * TILE_ROWS
    half = amp_ref.shape[2]
    width = high_ref.shape[1]
    step = pl.program_id(0)

    @pl.when(step == 0)
    def _():
        for i in range(ranks):
            at = pl.ds(i * TILE_ROWS, TILE_ROWS)
            low_at = pl.ds(rows + i * TILE_ROWS, TILE_ROWS)
            for core in range(CORES):
                value = amp_ref[source_ref[i] * CORES + core]
                high = value.astype(jnp.bfloat16)
                columns = pl.ds(core * half, half)
                pair_ref[at, columns] = high
                pair_ref[low_at, columns] = (value - high.astype(jnp.float32)).astype(jnp.bfloat16)

    total_ref[...] = jnp.zeros_like(total_ref)
    for k in range(high_ref.shape[0] // TILE):
        @pl.when(flag_ref[k, step * width // TILE] != 0)
        def _():
            deep = pl.ds(k * TILE, TILE)
            both = jnp.dot(pair_ref[:, deep], high_ref[deep, :], preferred_element_type=jnp.float32)
            cross = jnp.dot(pair_ref[:rows, deep], low_ref[deep, :], preferred_element_type=jnp.float32)
            total_ref[...] += both[:rows] + (both[rows:] + cross)
    for i in range(ranks):
        out_refs[i][...] = total_ref[pl.ds(i * TILE_ROWS, TILE_ROWS), :]


def product(source, int_tiles, gathered, high, low):
    ranks = source.shape[0]
    depth, width = high.shape
    rows = ranks * TILE_ROWS
    columns = TILE // 2
    return pl.pallas_call(
        functools.partial(product_kernel, ranks),
        out_shape=[jax.ShapeDtypeStruct((TILE_ROWS, width), jnp.float32)] * ranks,
        grid_spec=pltpu.PrefetchScalarGridSpec(
            num_scalar_prefetch=2,
            grid=(width // columns,),
            in_specs=[
                pl.BlockSpec(gathered.shape, lambda i, *_: (0, 0, 0), pipeline_mode=pl.Buffered(1)),
                pl.BlockSpec((depth, columns), lambda i, *_: (0, i)),
                pl.BlockSpec((depth, columns), lambda i, *_: (0, i)),
            ],
            out_specs=[pl.BlockSpec((TILE_ROWS, columns), lambda i, *_: (0, i))] * ranks,
            scratch_shapes=[
                pltpu.VMEM((2 * rows, depth), jnp.bfloat16),
                pltpu.VMEM((rows, columns), jnp.float32),
            ],
        ),
        compiler_params=pltpu.CompilerParams(vmem_limit_bytes=VMEM_BYTES),
        cost_estimate=pl.CostEstimate(
            flops=6 * rows * depth * width, bytes_accessed=4 * depth * width, transcendentals=0
        ),
    )(source, int_tiles, gathered, high, low)


def finish_kernel(ranks, slot_ref, *refs):
    parts, (term_ref, denominator_ref) = refs[:ranks], refs[ranks : ranks + 2]
    total = parts[0][...]
    for part in parts[1:]:
        total = total + part[...]
    refs[-1][...] = (total + term_ref[...]) / denominator_ref[...]


def finish(slot, parts, other_terms, denominators, update):
    ranks = len(parts)
    width = other_terms.shape[1]
    columns = TILE
    part = pl.BlockSpec((TILE_ROWS, columns), lambda i, slot: (0, i))
    owned = pl.BlockSpec((TILE_ROWS, columns), lambda i, slot: (slot[0], i))
    before = [] if update is None else [update]
    return pl.pallas_call(
        functools.partial(finish_kernel, ranks),
        out_shape=jax.ShapeDtypeStruct(other_terms.shape, jnp.float32),
        grid_spec=pltpu.PrefetchScalarGridSpec(
            num_scalar_prefetch=1,
            grid=(width // columns,),
            in_specs=[part] * ranks + [owned, owned] + [pl.BlockSpec(memory_space=pl.ANY)] * len(before),
            out_specs=owned,
        ),
        input_output_aliases={ranks + 3: 0} if before else {},
        cost_estimate=pl.CostEstimate(
            flops=0, bytes_accessed=4 * (ranks + 3) * TILE_ROWS * width, transcendentals=0
        ),
    )(slot, *parts, other_terms, denominators, *before)


def in_rounds(chips, rounds, amplitudes, amp_tiles, integrals, int_tiles, owner_tiles, other_terms, denominators):
    rank = lax.axis_index("cd")
    place = lax.axis_index("ab")
    core = (place % CORES).astype(jnp.int32).reshape(1)
    chip = place // CORES
    swapped = lax.ppermute(
        other_half(core, amp_tiles, amplitudes), "ab", [(i, i ^ 1) for i in range(chips * CORES)]
    )
    pick, source, slot = plan(owner_tiles, chips, rounds)
    high, low = split(integrals)
    peers = rank ^ jnp.arange(chips, dtype=jnp.int32)
    update = None
    for r in range(rounds):
        mine = lax.dynamic_slice(pick, (r * chips + chip,), (1,))
        gathered = lax.all_gather(pack(core, mine, amp_tiles, amplitudes, swapped), "ab", axis=0)
        parts = product(source[r * chips + peers], int_tiles, gathered, high, low)
        parts = [parts[0]] + [
            lax.ppermute(parts[d], "cd", [(c, c ^ d) for c in range(chips)]) for d in range(1, chips)
        ]
        here = lax.dynamic_slice(slot, (r * chips + rank,), (1,))
        update = finish(here, parts, other_terms, denominators, update)
    return update


def solution(mesh):
    ranks, places = mesh.shape["cd"], mesh.shape["ab"]

    def on_device(amplitudes, amp_tiles, integrals, int_tiles, owner_tiles, other_terms, denominators):
        args = (amplitudes, amp_tiles, integrals, int_tiles, owner_tiles, other_terms, denominators)
        tiles = owner_tiles.shape[0]
        chips = places // CORES
        rounds = tiles // chips
        whole = places % CORES == 0 and tiles == chips * rounds and amplitudes.shape[1] % (CORES * TILE) == 0
        if whole and chips == ranks and ranks in (2, 4):
            return in_rounds(chips, rounds, *args)
        return plain(*args)

    return jax.shard_map(
        on_device,
        mesh=mesh,
        in_specs=(
            P("ab", "cd"),
            P("ab", "cd"),
            P("cd", "ab"),
            P("cd", "ab"),
            P(),
            P("cd", "ab"),
            P("cd", "ab"),
        ),
        out_specs=P("cd", "ab"),
        check_vma=False,
    )
```

```python
import functools
import itertools

import jax
import jax.numpy as jnp
from jax import lax
from jax.experimental import pallas as pl
from jax.experimental.pallas import tpu as pltpu
from jax.sharding import PartitionSpec as P

TILE = 1024
TILE_ROWS = 128
CORES = 2
VMEM_BYTES = 58 * 1024 * 1024
CHAINS = 2
RANKS = (((0, 2), (1, 3)), ((0, 1), (2, 3)))


def spread_tiles(tile_flags, row_span, col_span):
    tile_rows, tile_cols = tile_flags.shape
    values = tile_flags.astype(jnp.float32)
    return jnp.broadcast_to(
        values[:, None, :, None], (tile_rows, row_span, tile_cols, col_span)
    ).reshape(tile_rows * row_span, tile_cols * col_span)


def plain(amplitudes, amp_tiles, integrals, int_tiles, owner_tiles, other_terms, denominators):
    masked_ints = integrals * spread_tiles(int_tiles, TILE, TILE)
    masked_amps = amplitudes * spread_tiles(amp_tiles, TILE_ROWS, TILE)
    tile_count = owner_tiles.shape[0]
    gathered = lax.all_gather(masked_amps, "ab", axis=0, tiled=True)
    partial_value = jnp.dot(
        gathered, masked_ints, precision=lax.Precision.HIGHEST, preferred_element_type=jnp.float32
    )
    col_width = partial_value.shape[1]
    partial_value = partial_value.reshape(tile_count, TILE_ROWS, col_width)[owner_tiles].reshape(
        tile_count * TILE_ROWS, col_width
    )
    owned = lax.psum_scatter(partial_value, "cd", scatter_dimension=0, tiled=True)
    return (owned + other_terms) / denominators


def plan_kernel(chips, rounds, owner_ref, here_ref, pick_ref, place_ref, slot_ref, inverse_ref):
    rank, chip = here_ref[0], here_ref[1]
    for q in range(chips * rounds):
        inverse_ref[owner_ref[q]] = q
    owner = [[inverse_ref[z * rounds + k] // rounds for k in range(rounds)] for z in range(chips)]
    left = [
        [sum((owner[z][k] == c).astype(jnp.int32) for k in range(rounds)) for c in range(chips)]
        for z in range(chips)
    ]
    used = [[jnp.int32(0)] * rounds for _ in range(chips)]
    for r in range(rounds):
        there = [[jnp.minimum(left[z][c], 1) for c in range(chips)] for z in range(chips)]
        code = jnp.int32(0)
        for order in itertools.permutations(range(chips)):
            fits = there[0][order[0]]
            for z in range(1, chips):
                fits = fits * there[z][order[z]]
            code = jnp.where(fits > 0, sum(c << (4 * z) for z, c in enumerate(order)), code)
        my_pick = jnp.int32(0)
        slot = jnp.int32(0)
        for z in range(chips):
            target = (code >> (4 * z)) & 15
            for c in range(chips):
                left[z][c] = left[z][c] - (target == c).astype(jnp.int32)
            pick = jnp.int32(0)
            for k in range(rounds):
                free = (owner[z][k] == target).astype(jnp.int32) * (1 - used[z][k])
                pick = jnp.where(free > 0, k, pick)
            for k in range(rounds):
                used[z][k] = jnp.maximum(used[z][k], (pick == k).astype(jnp.int32))
            my_pick = jnp.where(chip == z, pick, my_pick)
            slot = jnp.where(target == rank, inverse_ref[z * rounds + pick] % rounds, slot)
            place_ref[r * chips + z] = target ^ rank
        pick_ref[r] = my_pick
        slot_ref[r] = slot


def plan(owner_tiles, here, chips, rounds):
    each = jax.ShapeDtypeStruct((rounds,), jnp.int32)
    smem = pl.BlockSpec(memory_space=pltpu.SMEM)
    return pl.pallas_call(
        functools.partial(plan_kernel, chips, rounds),
        out_shape=(each, jax.ShapeDtypeStruct((rounds * chips,), jnp.int32), each),
        in_specs=[smem, smem],
        out_specs=(smem, smem, smem),
        scratch_shapes=[pltpu.SMEM((chips * rounds,), jnp.int32)],
    )(owner_tiles, here)


def half_kernel(core_ref, flag_ref, amp_ref, out_ref):
    tiles = flag_ref.shape[1] // CORES
    flag = flag_ref[pl.program_id(0), (1 - core_ref[0]) * tiles + pl.program_id(1)]
    out_ref[...] = amp_ref[...] * flag.astype(jnp.float32)


def other_half(core, amp_tiles, amplitudes):
    rows, depth = amplitudes.shape
    tiles = depth // TILE // CORES
    return pl.pallas_call(
        half_kernel,
        out_shape=jax.ShapeDtypeStruct((rows, depth // CORES), jnp.float32),
        grid_spec=pltpu.PrefetchScalarGridSpec(
            num_scalar_prefetch=2,
            grid=(rows // TILE_ROWS, tiles),
            in_specs=[
                pl.BlockSpec((TILE_ROWS, TILE), lambda i, j, core, flags: (i, (1 - core[0]) * tiles + j))
            ],
            out_specs=pl.BlockSpec((TILE_ROWS, TILE), lambda i, j, core, flags: (i, j)),
        ),
    )(core, amp_tiles, amplitudes)


def pack_kernel(r, core_ref, pick_ref, flag_ref, amp_ref, swapped_ref, out_ref):
    tiles = flag_ref.shape[1] // CORES
    per_core = flag_ref.shape[0]
    core = core_ref[0]
    pick = pick_ref[r]
    mine = pick // per_core == core

    @pl.when(mine)
    def _():
        for j in range(tiles):
            flag = flag_ref[pick % per_core, core * tiles + j].astype(jnp.float32)
            columns = pl.ds(j * TILE, TILE)
            out_ref[:, columns] = amp_ref[:, columns] * flag

    @pl.when(jnp.logical_not(mine))
    def _():
        out_ref[...] = swapped_ref[...]


def pack(r, core, pick, amp_tiles, amplitudes, swapped):
    per_core = amp_tiles.shape[0]
    half = swapped.shape[1]
    return pl.pallas_call(
        functools.partial(pack_kernel, r),
        out_shape=jax.ShapeDtypeStruct((TILE_ROWS, half), jnp.float32),
        grid_spec=pltpu.PrefetchScalarGridSpec(
            num_scalar_prefetch=3,
            grid=(1,),
            in_specs=[
                pl.BlockSpec((TILE_ROWS, half), lambda i, core, pick, flags: (pick[r] % per_core, core[0])),
                pl.BlockSpec((TILE_ROWS, half), lambda i, core, pick, flags: (pick[r] % per_core, 0)),
            ],
            out_specs=pl.BlockSpec((TILE_ROWS, half), lambda i, core, pick, flags: (0, 0)),
        ),
    )(core, pick, amp_tiles, amplitudes, swapped)


def split_kernel(value_ref, high_ref, low_ref):
    value = value_ref[...]
    high = value.astype(jnp.bfloat16)
    high_ref[...] = high
    low_ref[...] = (value - high.astype(jnp.float32)).astype(jnp.bfloat16)


def split(integrals):
    depth, width = integrals.shape
    rows = TILE // 2
    block = pl.BlockSpec((rows, width), lambda i: (i, 0))
    half = jax.ShapeDtypeStruct((depth, width), jnp.bfloat16)
    return pl.pallas_call(
        split_kernel,
        out_shape=(half, half),
        grid=(depth // rows,),
        in_specs=[block],
        out_specs=(block, block),
        compiler_params=pltpu.CompilerParams(vmem_limit_bytes=VMEM_BYTES),
        cost_estimate=pl.CostEstimate(flops=0, bytes_accessed=8 * depth * width, transcendentals=0),
    )(integrals)


def product_kernel(r, first, ranks, core_ref, place_ref, flag_ref, mine_ref, other_ref, high_ref, low_ref, *refs):
    out_refs, (pair_ref, total_ref) = refs[: 2 * CHAINS], refs[2 * CHAINS :]
    rows = ranks * TILE_ROWS
    half = mine_ref.shape[2]
    width = high_ref.shape[1]
    step = pl.program_id(0)

    @pl.when(step == 0)
    def _():
        for z in range(ranks):
            at = pl.multiple_of(place_ref[r * ranks + z] * TILE_ROWS, TILE_ROWS)
            for away, amp_ref in enumerate((mine_ref, other_ref)):
                value = amp_ref[z]
                high = value.astype(jnp.bfloat16)
                columns = pl.ds(pl.multiple_of((core_ref[0] ^ away) * half, half), half)
                pair_ref[pl.ds(at, TILE_ROWS), columns] = high
                pair_ref[pl.ds(rows + at, TILE_ROWS), columns] = (value - high.astype(jnp.float32)).astype(
                    jnp.bfloat16
                )

    total_ref[...] = jnp.zeros_like(total_ref)
    for k in range(high_ref.shape[0] // TILE):
        @pl.when(flag_ref[k, (first + step) * width // TILE] != 0)
        def _():
            deep = pl.ds(k * TILE, TILE)
            both = jnp.dot(pair_ref[:, deep], high_ref[deep, :], preferred_element_type=jnp.float32)
            cross = jnp.dot(pair_ref[:rows, deep], low_ref[deep, :], preferred_element_type=jnp.float32)
            total_ref[...] += both[:rows] + (both[rows:] + cross)
    share = width // CHAINS
    for chain, (kept, sent) in enumerate(RANKS):
        columns = pl.ds(chain * share, share)
        for ref, peers in ((out_refs[2 * chain], kept), (out_refs[2 * chain + 1], sent)):
            for i, peer in enumerate(peers):
                ref[i] = total_ref[pl.ds(peer * TILE_ROWS, TILE_ROWS), columns]


def product(r, piece, pieces, core, place, int_tiles, mine, other, high, low):
    ranks = mine.shape[0]
    depth, width = high.shape
    rows = ranks * TILE_ROWS
    columns = TILE // 2
    share = columns // CHAINS
    steps = width // columns // pieces
    amp = pl.BlockSpec(mine.shape, lambda i, *_: (0, 0, 0), pipeline_mode=pl.Buffered(1))
    integral = pl.BlockSpec((depth, columns), lambda i, *_: (0, piece * steps + i))
    return pl.pallas_call(
        functools.partial(product_kernel, r, piece * steps, ranks),
        out_shape=[jax.ShapeDtypeStruct((2, TILE_ROWS, share * steps), jnp.float32)] * (2 * CHAINS),
        grid_spec=pltpu.PrefetchScalarGridSpec(
            num_scalar_prefetch=3,
            grid=(steps,),
            in_specs=[amp, amp, integral, integral],
            out_specs=[pl.BlockSpec((2, TILE_ROWS, share), lambda i, *_: (0, 0, i))] * (2 * CHAINS),
            scratch_shapes=[
                pltpu.VMEM((2 * rows, depth), jnp.bfloat16),
                pltpu.VMEM((rows, columns), jnp.float32),
            ],
        ),
        compiler_params=pltpu.CompilerParams(vmem_limit_bytes=VMEM_BYTES),
        cost_estimate=pl.CostEstimate(
            flops=6 * rows * depth * width // pieces, bytes_accessed=4 * depth * width // pieces, transcendentals=0
        ),
    )(core, place, int_tiles, mine, other, high, low)


def relay_kernel(*refs):
    for chain in range(CHAINS):
        refs[2 * CHAINS + chain][...] = refs[2 * chain][0] + refs[2 * chain + 1][0]


def relay(kept, heard):
    _, rows, width = kept[0].shape
    passed = pl.BlockSpec((1, rows, width), lambda i: (1, 0, 0))
    out = jax.ShapeDtypeStruct((rows, width), jnp.float32)
    return pl.pallas_call(
        relay_kernel,
        out_shape=[out] * CHAINS,
        grid=(1,),
        in_specs=[passed] * (2 * CHAINS),
        out_specs=[pl.BlockSpec((rows, width), lambda i: (0, 0))] * CHAINS,
    )(*[array for pair in zip(kept, heard) for array in pair])


def finish_kernel(columns, *refs):
    refs = refs[1:]
    parts, (term_ref, denominator_ref), out_ref = refs[: 3 * CHAINS], refs[3 * CHAINS : 3 * CHAINS + 2], refs[-1]
    share = columns // CHAINS
    for block in range(term_ref.shape[1] // columns):
        for chain in range(CHAINS):
            kept, heard, relayed = parts[3 * chain : 3 * chain + 3]
            source = pl.ds(block * share, share)
            target = pl.ds(block * columns + chain * share, share)
            total = kept[0, :, source] + heard[0, :, source] + relayed[:, source]
            out_ref[:, target] = (total + term_ref[:, target]) / denominator_ref[:, target]


def finish(r, piece, slot, kept, heard, relayed, other_terms, denominators, update):
    share = kept[0].shape[2]
    width = share * CHAINS
    first = pl.BlockSpec((1, TILE_ROWS, share), lambda i, slot: (0, 0, 0))
    whole = pl.BlockSpec((TILE_ROWS, share), lambda i, slot: (0, 0))
    owned = pl.BlockSpec((TILE_ROWS, width), lambda i, slot: (slot[r], piece))
    before = [] if update is None else [update]
    return pl.pallas_call(
        functools.partial(finish_kernel, TILE // 2),
        out_shape=jax.ShapeDtypeStruct(other_terms.shape, jnp.float32),
        grid_spec=pltpu.PrefetchScalarGridSpec(
            num_scalar_prefetch=1,
            grid=(1,),
            in_specs=[first, first, whole] * CHAINS
            + [owned, owned]
            + [pl.BlockSpec(memory_space=pl.ANY)] * len(before),
            out_specs=owned,
        ),
        input_output_aliases={3 * CHAINS + 3: 0} if before else {},
        cost_estimate=pl.CostEstimate(flops=0, bytes_accessed=24 * TILE_ROWS * width, transcendentals=0),
    )(
        slot,
        *[array for chain in zip(kept, heard, relayed) for array in chain],
        other_terms,
        denominators,
        *before,
    )


def in_rounds(chips, rounds, amplitudes, amp_tiles, integrals, int_tiles, owner_tiles, other_terms, denominators):
    rank = lax.axis_index("cd").astype(jnp.int32)
    spot = lax.axis_index("ab").astype(jnp.int32)
    core = (spot % CORES).reshape(1)
    spots = chips * CORES
    siblings = [(i, i ^ 1) for i in range(spots)]
    same_core = [list(range(i, spots, CORES)) for i in range(CORES)]
    swapped = lax.ppermute(other_half(core, amp_tiles, amplitudes), "ab", siblings)
    pick, place, slot = plan(owner_tiles, jnp.stack([rank, spot // CORES]), chips, rounds)
    high, low = split(integrals)
    owns = [pack(r, core, pick, amp_tiles, amplitudes, swapped) for r in range(rounds)]
    gathered = [lax.all_gather(own, "ab", axis=0, axis_index_groups=same_core) for own in owns]
    def swap(sent, peers):
        return [lax.ppermute(array, "cd", [(c, c ^ peer) for c in range(chips)]) for array, peer in zip(sent, peers)]

    terms = (other_terms, denominators)
    update = waiting = None
    for r in range(rounds):
        if r == 0:
            mine, high, low, *_ = lax.optimization_barrier((gathered[r], high, low, *owns))
        else:
            mine, onward, update = lax.optimization_barrier((gathered[r], onward, update))
        other = lax.ppermute(mine, "ab", siblings)
        pieces = 2 if r == rounds - 1 else 1
        sums = []
        for piece in range(pieces):
            parts = product(r, piece, pieces, core, place, int_tiles, mine, other, high, low)
            if waiting is not None:
                parts, relayed = lax.optimization_barrier((parts, waiting[-1]))
                update = finish(*waiting[:-1], relayed, *terms, update)
                waiting = None
            if piece > 0:
                parts, heard = lax.optimization_barrier((parts, sums[-1][1]))
                sums[-1] = (sums[-1][0], heard)
            sums.append((parts[0::2], swap(parts[1::2], (1, 2))))
        for piece, (kept, heard) in enumerate(sums):
            if piece > 0:
                heard, update = lax.optimization_barrier((heard, update))
            onward = relay(kept, heard)
            relayed = swap(onward, (2, 1))
            if piece < pieces - 1 or r == rounds - 1:
                sums[piece] = (r, piece, slot, kept, heard, relayed)
            else:
                waiting = (r, piece, slot, kept, heard, relayed)
    for ready in sums:
        update = finish(*ready, *terms, update)
    return update


def solution(mesh):
    ranks, places = mesh.shape["cd"], mesh.shape["ab"]

    def on_device(amplitudes, amp_tiles, integrals, int_tiles, owner_tiles, other_terms, denominators):
        args = (amplitudes, amp_tiles, integrals, int_tiles, owner_tiles, other_terms, denominators)
        tiles = owner_tiles.shape[0]
        chips = places // CORES
        rounds = tiles // chips
        whole = places % CORES == 0 and tiles == chips * rounds and amplitudes.shape[1] % (CORES * TILE) == 0
        if whole and chips == ranks and ranks == 4:
            return in_rounds(chips, rounds, *args)
        return plain(*args)

    return jax.shard_map(
        on_device,
        mesh=mesh,
        in_specs=(
            P("ab", "cd"),
            P("ab", "cd"),
            P("cd", "ab"),
            P("cd", "ab"),
            P(),
            P("cd", "ab"),
            P("cd", "ab"),
        ),
        out_specs=P("cd", "ab"),
        check_vma=False,
    )
```

```python
import functools
import itertools

import jax
import jax.numpy as jnp
from jax import lax
from jax.experimental import pallas as pl
from jax.experimental.pallas import tpu as pltpu
from jax.sharding import PartitionSpec as P

TILE = 1024
TILE_ROWS = 128
CORES = 2
VMEM_BYTES = 40 * 1024 * 1024
COLUMNS = 256
SMALL = pl.CostEstimate(flops=1, bytes_accessed=1, transcendentals=0)
CHAINS = 2
RANKS = (((0, 2), (1, 3)), ((0, 1), (2, 3)))


def spread_tiles(tile_flags, row_span, col_span):
    tile_rows, tile_cols = tile_flags.shape
    values = tile_flags.astype(jnp.float32)
    return jnp.broadcast_to(
        values[:, None, :, None], (tile_rows, row_span, tile_cols, col_span)
    ).reshape(tile_rows * row_span, tile_cols * col_span)


def plain(amplitudes, amp_tiles, integrals, int_tiles, owner_tiles, other_terms, denominators):
    masked_ints = integrals * spread_tiles(int_tiles, TILE, TILE)
    masked_amps = amplitudes * spread_tiles(amp_tiles, TILE_ROWS, TILE)
    tile_count = owner_tiles.shape[0]
    gathered = lax.all_gather(masked_amps, "ab", axis=0, tiled=True)
    partial_value = jnp.dot(
        gathered, masked_ints, precision=lax.Precision.HIGHEST, preferred_element_type=jnp.float32
    )
    col_width = partial_value.shape[1]
    partial_value = partial_value.reshape(tile_count, TILE_ROWS, col_width)[owner_tiles].reshape(
        tile_count * TILE_ROWS, col_width
    )
    owned = lax.psum_scatter(partial_value, "cd", scatter_dimension=0, tiled=True)
    return (owned + other_terms) / denominators


def plan_kernel(chips, rounds, owner_ref, here_ref, pick_ref, place_ref, slot_ref, inverse_ref):
    rank, chip = here_ref[0], here_ref[1]
    for q in range(chips * rounds):
        inverse_ref[owner_ref[q]] = q
    owner = [[inverse_ref[z * rounds + k] // rounds for k in range(rounds)] for z in range(chips)]
    left = [
        [sum((owner[z][k] == c).astype(jnp.int32) for k in range(rounds)) for c in range(chips)]
        for z in range(chips)
    ]
    used = [[jnp.int32(0)] * rounds for _ in range(chips)]
    for r in range(rounds):
        there = [[jnp.minimum(left[z][c], 1) for c in range(chips)] for z in range(chips)]
        code = jnp.int32(0)
        for order in itertools.permutations(range(chips)):
            fits = there[0][order[0]]
            for z in range(1, chips):
                fits = fits * there[z][order[z]]
            code = jnp.where(fits > 0, sum(c << (4 * z) for z, c in enumerate(order)), code)
        my_pick = jnp.int32(0)
        slot = jnp.int32(0)
        for z in range(chips):
            target = (code >> (4 * z)) & 15
            for c in range(chips):
                left[z][c] = left[z][c] - (target == c).astype(jnp.int32)
            pick = jnp.int32(0)
            for k in range(rounds):
                free = (owner[z][k] == target).astype(jnp.int32) * (1 - used[z][k])
                pick = jnp.where(free > 0, k, pick)
            for k in range(rounds):
                used[z][k] = jnp.maximum(used[z][k], (pick == k).astype(jnp.int32))
            my_pick = jnp.where(chip == z, pick, my_pick)
            slot = jnp.where(target == rank, inverse_ref[z * rounds + pick] % rounds, slot)
            distance = (chip + (chips - z)) % chips
            place_ref[r * chips + distance] = target ^ rank if r == rounds - 1 else target
        pick_ref[r] = my_pick
        slot_ref[r] = slot


def plan(owner_tiles, here, chips, rounds):
    each = jax.ShapeDtypeStruct((rounds,), jnp.int32)
    smem = pl.BlockSpec(memory_space=pltpu.SMEM)
    return pl.pallas_call(
        functools.partial(plan_kernel, chips, rounds),
        out_shape=(each, jax.ShapeDtypeStruct((rounds * chips,), jnp.int32), each),
        in_specs=[smem, smem],
        out_specs=(smem, smem, smem),
        scratch_shapes=[pltpu.SMEM((chips * rounds,), jnp.int32)],
    )(owner_tiles, here)


def half_kernel(core_ref, flag_ref, amp_ref, out_ref):
    tiles = flag_ref.shape[1] // CORES
    flag = flag_ref[pl.program_id(0), (1 - core_ref[0]) * tiles + pl.program_id(1)]
    out_ref[...] = amp_ref[...] * flag.astype(jnp.float32)


def other_half(core, amp_tiles, amplitudes):
    rows, depth = amplitudes.shape
    tiles = depth // TILE // CORES
    return pl.pallas_call(
        half_kernel,
        out_shape=jax.ShapeDtypeStruct((rows, depth // CORES), jnp.float32),
        grid_spec=pltpu.PrefetchScalarGridSpec(
            num_scalar_prefetch=2,
            grid=(rows // TILE_ROWS, tiles),
            in_specs=[
                pl.BlockSpec((TILE_ROWS, TILE), lambda i, j, core, flags: (i, (1 - core[0]) * tiles + j))
            ],
            out_specs=pl.BlockSpec((TILE_ROWS, TILE), lambda i, j, core, flags: (i, j)),
        ),
    )(core, amp_tiles, amplitudes)


def pack_kernel(r, core_ref, pick_ref, flag_ref, amp_ref, swapped_ref, out_ref):
    tiles = flag_ref.shape[1] // CORES
    per_core = flag_ref.shape[0]
    core = core_ref[0]
    pick = pick_ref[r]
    mine = pick // per_core == core

    @pl.when(mine)
    def _():
        for j in range(tiles):
            flag = flag_ref[pick % per_core, core * tiles + j].astype(jnp.float32)
            columns = pl.ds(j * TILE, TILE)
            out_ref[:, columns] = amp_ref[:, columns] * flag

    @pl.when(jnp.logical_not(mine))
    def _():
        out_ref[...] = swapped_ref[...]


def pack(r, core, pick, amp_tiles, amplitudes, swapped):
    per_core = amp_tiles.shape[0]
    half = swapped.shape[1]
    return pl.pallas_call(
        functools.partial(pack_kernel, r),
        out_shape=jax.ShapeDtypeStruct((TILE_ROWS, half), jnp.float32),
        grid_spec=pltpu.PrefetchScalarGridSpec(
            num_scalar_prefetch=3,
            grid=(1,),
            in_specs=[
                pl.BlockSpec((TILE_ROWS, half), lambda i, core, pick, flags: (pick[r] % per_core, core[0])),
                pl.BlockSpec((TILE_ROWS, half), lambda i, core, pick, flags: (pick[r] % per_core, 0)),
            ],
            out_specs=pl.BlockSpec((TILE_ROWS, half), lambda i, core, pick, flags: (0, 0)),
        ),
        cost_estimate=SMALL,
    )(core, pick, amp_tiles, amplitudes, swapped)


def split_kernel(value_ref, high_ref, low_ref):
    value = value_ref[...]
    high = value.astype(jnp.bfloat16)
    high_ref[...] = high
    low_ref[...] = (value - high.astype(jnp.float32)).astype(jnp.bfloat16)


def split(integrals):
    depth, width = integrals.shape
    rows = TILE // 2
    block = pl.BlockSpec((rows, width), lambda i: (i, 0))
    half = jax.ShapeDtypeStruct((depth, width), jnp.bfloat16)
    return pl.pallas_call(
        split_kernel,
        out_shape=(half, half),
        grid=(depth // rows,),
        in_specs=[block],
        out_specs=(block, block),
        compiler_params=pltpu.CompilerParams(vmem_limit_bytes=VMEM_BYTES),
        cost_estimate=pl.CostEstimate(flops=0, bytes_accessed=16 * depth * width, transcendentals=0),
    )(integrals)


def product_kernel(r, first, ranks, chained, core_ref, place_ref, flag_ref, *refs):
    amp_refs, (high_ref, low_ref), refs = refs[: CORES * ranks], refs[CORES * ranks :][:2], refs[CORES * ranks + 2 :]
    out_refs, (pair_ref, total_ref) = refs[:-2], refs[-2:]
    rows = ranks * TILE_ROWS
    half = amp_refs[0].shape[1]
    width = high_ref.shape[1]
    step = pl.program_id(0)

    @pl.when(step == 0)
    def _():
        for away in range(CORES):
            columns = pl.ds(pl.multiple_of((core_ref[0] ^ away) * half, half), half)
            for d in range(ranks):
                at = pl.multiple_of(place_ref[r * ranks + d] * TILE_ROWS, TILE_ROWS)
                value = amp_refs[away * ranks + d][...]
                high = value.astype(jnp.bfloat16)
                pair_ref[pl.ds(at, TILE_ROWS), columns] = high
                pair_ref[pl.ds(rows + at, TILE_ROWS), columns] = (value - high.astype(jnp.float32)).astype(
                    jnp.bfloat16
                )

    total_ref[...] = jnp.zeros_like(total_ref)
    for k in range(high_ref.shape[0] // TILE):
        @pl.when(flag_ref[k, (first + step) * width // TILE] != 0)
        def _():
            deep = pl.ds(k * TILE, TILE)
            both = jnp.dot(pair_ref[:, deep], high_ref[deep, :], preferred_element_type=jnp.float32)
            cross = jnp.dot(pair_ref[:rows, deep], low_ref[deep, :], preferred_element_type=jnp.float32)
            total_ref[...] += both[:rows] + (both[rows:] + cross)
    if not chained:
        out_refs[0][...] = total_ref[...]
        return
    share = width // CHAINS
    for chain, (kept, sent) in enumerate(RANKS):
        columns = pl.ds(chain * share, share)
        for ref, peers in ((out_refs[2 * chain], kept), (out_refs[2 * chain + 1], sent)):
            for i, peer in enumerate(peers):
                ref[i] = total_ref[pl.ds(peer * TILE_ROWS, TILE_ROWS), columns]


def product(r, piece, pieces, chained, core, place, int_tiles, mine, other, high, low):
    ranks = len(mine)
    depth, width = high.shape
    rows = ranks * TILE_ROWS
    columns = COLUMNS
    share = columns // CHAINS
    steps = width // columns // pieces
    amp = pl.BlockSpec(mine[0].shape, lambda i, *_: (0, 0), pipeline_mode=pl.Buffered(1))
    integral = pl.BlockSpec((depth, columns), lambda i, *_: (0, piece * steps + i))
    if chained:
        out_shape = [jax.ShapeDtypeStruct((2, TILE_ROWS, share * steps), jnp.float32)] * (2 * CHAINS)
        out_specs = [pl.BlockSpec((2, TILE_ROWS, share), lambda i, *_: (0, 0, i))] * (2 * CHAINS)
    else:
        out_shape = [jax.ShapeDtypeStruct((rows, columns * steps), jnp.float32)]
        out_specs = [pl.BlockSpec((rows, columns), lambda i, *_: (0, i))]
    return pl.pallas_call(
        functools.partial(product_kernel, r, piece * steps, ranks, chained),
        out_shape=out_shape,
        grid_spec=pltpu.PrefetchScalarGridSpec(
            num_scalar_prefetch=3,
            grid=(steps,),
            in_specs=[amp] * (CORES * ranks) + [integral, integral],
            out_specs=out_specs,
            scratch_shapes=[
                pltpu.VMEM((2 * rows, depth), jnp.bfloat16),
                pltpu.VMEM((rows, columns), jnp.float32),
            ],
        ),
        compiler_params=pltpu.CompilerParams(vmem_limit_bytes=VMEM_BYTES),
        cost_estimate=pl.CostEstimate(
            flops=6 * rows * depth * width, bytes_accessed=4 * depth * width, transcendentals=0
        ),
    )(core, place, int_tiles, *mine, *other, high, low)


def relay_kernel(*refs):
    for chain in range(CHAINS):
        refs[2 * CHAINS + chain][...] = refs[2 * chain][0] + refs[2 * chain + 1][0]


def relay(kept, heard):
    _, rows, width = kept[0].shape
    passed = pl.BlockSpec((1, rows, width), lambda i: (1, 0, 0))
    out = jax.ShapeDtypeStruct((rows, width), jnp.float32)
    return pl.pallas_call(
        relay_kernel,
        out_shape=[out] * CHAINS,
        grid=(1,),
        in_specs=[passed] * (2 * CHAINS),
        out_specs=[pl.BlockSpec((rows, width), lambda i: (0, 0))] * CHAINS,
    )(*[array for pair in zip(kept, heard) for array in pair])


def finish_kernel(columns, *refs):
    refs = refs[1:]
    parts, (term_ref, denominator_ref), out_ref = refs[: 3 * CHAINS], refs[3 * CHAINS : 3 * CHAINS + 2], refs[-1]
    share = columns // CHAINS
    for block in range(term_ref.shape[1] // columns):
        for chain in range(CHAINS):
            kept, heard, relayed = parts[3 * chain : 3 * chain + 3]
            source = pl.ds(block * share, share)
            target = pl.ds(block * columns + chain * share, share)
            total = kept[0, :, source] + heard[0, :, source] + relayed[:, source]
            out_ref[:, target] = (total + term_ref[:, target]) / denominator_ref[:, target]


def finish(r, piece, slot, kept, heard, relayed, other_terms, denominators, update):
    share = kept[0].shape[2]
    width = share * CHAINS
    first = pl.BlockSpec((1, TILE_ROWS, share), lambda i, slot: (0, 0, 0))
    whole = pl.BlockSpec((TILE_ROWS, share), lambda i, slot: (0, 0))
    owned = pl.BlockSpec((TILE_ROWS, width), lambda i, slot: (slot[r], piece))
    before = [] if update is None else [update]
    return pl.pallas_call(
        functools.partial(finish_kernel, COLUMNS),
        out_shape=jax.ShapeDtypeStruct(other_terms.shape, jnp.float32),
        grid_spec=pltpu.PrefetchScalarGridSpec(
            num_scalar_prefetch=1,
            grid=(1,),
            in_specs=[first, first, whole] * CHAINS
            + [owned, owned]
            + [pl.BlockSpec(memory_space=pl.ANY)] * len(before),
            out_specs=owned,
        ),
        input_output_aliases={3 * CHAINS + 3: 0} if before else {},
        cost_estimate=SMALL,
    )(
        slot,
        *[array for chain in zip(kept, heard, relayed) for array in chain],
        other_terms,
        denominators,
        *before,
    )


def settle_kernel(slot_ref, owned_ref, term_ref, denominator_ref, *refs):
    refs[-1][...] = (owned_ref[...] + term_ref[...]) / denominator_ref[...]


def settle(r, slot, owned, other_terms, denominators, update):
    width = owned.shape[1]
    columns = min(TILE, width)
    here = pl.BlockSpec((TILE_ROWS, columns), lambda i, slot: (slot[r], i))
    before = [] if update is None else [update]
    return pl.pallas_call(
        settle_kernel,
        out_shape=jax.ShapeDtypeStruct(other_terms.shape, jnp.float32),
        grid_spec=pltpu.PrefetchScalarGridSpec(
            num_scalar_prefetch=1,
            grid=(width // columns,),
            in_specs=[pl.BlockSpec((TILE_ROWS, columns), lambda i, slot: (0, i)), here, here]
            + [pl.BlockSpec(memory_space=pl.ANY)] * len(before),
            out_specs=here,
        ),
        input_output_aliases={4: 0} if before else {},
        cost_estimate=SMALL,
    )(slot, owned, other_terms, denominators, *before)


def in_rounds(chips, rounds, amplitudes, amp_tiles, integrals, int_tiles, owner_tiles, other_terms, denominators):
    rank = lax.axis_index("cd").astype(jnp.int32)
    spot = lax.axis_index("ab").astype(jnp.int32)
    core = (spot % CORES).reshape(1)
    spots = chips * CORES

    def across(array):
        return lax.ppermute(array, "ab", [(i, i ^ 1) for i in range(spots)])

    def shifts(array):
        return [
            lax.ppermute(array, "ab", [(i, (i + CORES * d) % spots) for i in range(spots)]) for d in range(1, chips)
        ]

    def swap(sent, peers):
        return [lax.ppermute(array, "cd", [(c, c ^ peer) for c in range(chips)]) for array, peer in zip(sent, peers)]

    swapped = across(other_half(core, amp_tiles, amplitudes))
    pick, place, slot = plan(owner_tiles, jnp.stack([rank, spot // CORES]), chips, rounds)
    high, low = split(integrals)
    owns = [pack(0, core, pick, amp_tiles, amplitudes, swapped)]
    pick, high, low = lax.optimization_barrier((pick, high, low))
    owns += [pack(r, core, pick, amp_tiles, amplitudes, swapped) for r in range(1, rounds)]
    terms = (other_terms, denominators)
    last = rounds - 1
    update = owned = None
    arrived = shifts(owns[0])
    for r in range(rounds):
        if r == 0:
            arrived, owns, high, low = lax.optimization_barrier((arrived, owns, high, low))
        else:
            arrived, parts, update = lax.optimization_barrier((arrived, parts, update))
        mine = [owns[r], *arrived]
        if r < last:
            begin, arrived = lax.optimization_barrier((owns[r + 1], arrived))
            following = shifts(begin)
        other = [*map(across, mine)]
        pieces = 1 if r < last else 2
        sums = []
        for piece in range(pieces):
            parts = product(r, piece, pieces, r == last, core, place, int_tiles, mine, other, high, low)
            if piece > 0:
                parts, heard = lax.optimization_barrier((parts, sums[-1][1]))
                sums[-1] = (sums[-1][0], heard)
            elif r > 0:
                parts, owned = lax.optimization_barrier((parts, owned))
                update = settle(r - 1, slot, owned, *terms, update)
            if r == last:
                sums.append((parts[0::2], swap(parts[1::2], (1, 2))))
        if r < last:
            owned = lax.psum_scatter(parts[0], "cd", scatter_dimension=0, tiled=True)
            arrived = following
    for piece, (kept, heard) in enumerate(sums):
        if piece > 0:
            heard, update = lax.optimization_barrier((heard, update))
        onward = relay(kept, heard)
        sums[piece] = (last, piece, slot, kept, heard, swap(onward, (2, 1)))
    for ready in sums:
        update = finish(*ready, *terms, update)
    return update


def solution(mesh):
    ranks, places = mesh.shape["cd"], mesh.shape["ab"]

    def on_device(amplitudes, amp_tiles, integrals, int_tiles, owner_tiles, other_terms, denominators):
        args = (amplitudes, amp_tiles, integrals, int_tiles, owner_tiles, other_terms, denominators)
        tiles = owner_tiles.shape[0]
        chips = places // CORES
        rounds = tiles // chips
        whole = places % CORES == 0 and tiles == chips * rounds and amplitudes.shape[1] % (CORES * TILE) == 0
        if whole and chips == ranks and ranks == 4:
            return in_rounds(chips, rounds, *args)
        return plain(*args)

    return jax.shard_map(
        on_device,
        mesh=mesh,
        in_specs=(
            P("ab", "cd"),
            P("ab", "cd"),
            P("cd", "ab"),
            P("cd", "ab"),
            P(),
            P("cd", "ab"),
            P("cd", "ab"),
        ),
        out_specs=P("cd", "ab"),
        check_vma=False,
    )
```

```python
import functools

import jax
import jax.numpy as jnp
from jax import lax
from jax.experimental import pallas as pl
from jax.experimental.pallas import tpu as pltpu
from jax.sharding import PartitionSpec as P

TILE = 1024
TILE_ROWS = 128
CORES = 2
VMEM_BYTES = 58 * 1024 * 1024
COLUMNS = 256
ROUNDS = 4
FIRST, AWAY, STAY, WHOSE = 0, 2, 4, 6
CHAINS = 2
RANKS = (((0, 2), (1, 3)), ((0, 1), (2, 3)))


def spread_tiles(tile_flags, row_span, col_span):
    tile_rows, tile_cols = tile_flags.shape
    values = tile_flags.astype(jnp.float32)
    return jnp.broadcast_to(
        values[:, None, :, None], (tile_rows, row_span, tile_cols, col_span)
    ).reshape(tile_rows * row_span, tile_cols * col_span)


def plain(amplitudes, amp_tiles, integrals, int_tiles, owner_tiles, other_terms, denominators):
    masked_ints = integrals * spread_tiles(int_tiles, TILE, TILE)
    masked_amps = amplitudes * spread_tiles(amp_tiles, TILE_ROWS, TILE)
    tile_count = owner_tiles.shape[0]
    gathered = lax.all_gather(masked_amps, "ab", axis=0, tiled=True)
    partial_value = jnp.dot(
        gathered, masked_ints, precision=lax.Precision.HIGHEST, preferred_element_type=jnp.float32
    )
    col_width = partial_value.shape[1]
    partial_value = partial_value.reshape(tile_count, TILE_ROWS, col_width)[owner_tiles].reshape(
        tile_count * TILE_ROWS, col_width
    )
    owned = lax.psum_scatter(partial_value, "cd", scatter_dimension=0, tiled=True)
    return (owned + other_terms) / denominators


def plan_kernel(devices, half, owner_ref, here_ref, take_ref, source_ref, slot_ref, *scratch):
    inverse_ref, color_ref, pair_ref, device_ref, late_ref = scratch
    rank, spot = here_ref[0], here_ref[1]
    ranks = devices * 2 // ROUNDS
    for q in range(2 * devices):
        inverse_ref[owner_ref[q]] = q
        color_ref[q] = -1
    for d in range(devices):
        late_ref[d] = -1

    def walk(first, colors_ref, after):
        def step(state):
            at, _ = state
            colors_ref[at] = 0
            colors_ref[at ^ 1] = 1
            following = after(at ^ 1)
            return following, colors_ref[following]

        lax.while_loop(lambda state: state[1] < 0, step, (jnp.int32(first), colors_ref[first]))

    for t in range(0, 2 * devices, 2):
        walk(t, color_ref, lambda u: owner_ref[inverse_ref[u] ^ 1])
    for c in range(ranks):
        for p in range(2):
            q = ROUNDS * c + 2 * p
            second = color_ref[owner_ref[q]]
            source_ref[p * ranks + (c ^ rank)] = owner_ref[q + second] >> 1
            group = 2 * c + p
            device = owner_ref[q + 1 - second] >> 1
            device_ref[group] = device
            pair_ref[device] = group

            @pl.when(rank == c)
            def _():
                slot_ref[p] = 2 * p + second
                slot_ref[2 + p] = 2 * p + 1 - second

    for d in range(0, devices, 2):
        walk(d, late_ref, lambda u: device_ref[pair_ref[u] ^ 1])
    for c in range(ranks):
        swap = late_ref[device_ref[2 * c]]
        for p in range(2):
            r = 2 + (swap ^ p)
            source_ref[r * ranks + (c ^ rank)] = device_ref[2 * c + p] >> 1

        @pl.when(jnp.logical_and(rank == c, swap != 0))
        def _():
            kept = slot_ref[2]
            slot_ref[2] = slot_ref[3]
            slot_ref[3] = kept

    early = color_ref[2 * spot]
    core = spot % CORES
    take_ref[FIRST] = early
    take_ref[FIRST + 1] = 0
    take_ref[AWAY] = 1 - early
    take_ref[AWAY + 1] = (1 - core) * half
    take_ref[STAY] = 1 - early
    take_ref[STAY + 1] = core * half
    take_ref[WHOSE] = late_ref[spot]


def plan(owner_tiles, here, devices, half):
    tiles = 2 * devices
    smem = pl.BlockSpec(memory_space=pltpu.SMEM)
    ints = jnp.int32
    return pl.pallas_call(
        functools.partial(plan_kernel, devices, half),
        out_shape=(
            jax.ShapeDtypeStruct((WHOSE + 1,), ints),
            jax.ShapeDtypeStruct((tiles,), ints),
            jax.ShapeDtypeStruct((ROUNDS,), ints),
        ),
        in_specs=[smem, smem],
        out_specs=(smem, smem, smem),
        scratch_shapes=[pltpu.SMEM((tiles,), ints)] * 2 + [pltpu.SMEM((devices,), ints)] * 3,
    )(owner_tiles, here)


def take_kernel(at, take_ref, flag_ref, amp_ref, out_ref):
    flag = flag_ref[take_ref[at], take_ref[at + 1] + pl.program_id(0)]
    out_ref[...] = amp_ref[...] * flag.astype(jnp.float32)


def take(at, tiles, where, amp_tiles, amplitudes):
    return pl.pallas_call(
        functools.partial(take_kernel, at),
        out_shape=jax.ShapeDtypeStruct((TILE_ROWS, tiles * TILE), jnp.float32),
        grid_spec=pltpu.PrefetchScalarGridSpec(
            num_scalar_prefetch=2,
            grid=(tiles,),
            in_specs=[
                pl.BlockSpec((TILE_ROWS, TILE), lambda j, where, flags: (where[at], where[at + 1] + j))
            ],
            out_specs=pl.BlockSpec((TILE_ROWS, TILE), lambda j, where, flags: (0, j)),
        ),
    )(where, amp_tiles, amplitudes)


def split_kernel(value_ref, high_ref, low_ref):
    value = value_ref[...]
    high = value.astype(jnp.bfloat16)
    high_ref[...] = high
    low_ref[...] = (value - high.astype(jnp.float32)).astype(jnp.bfloat16)


def split(integrals):
    depth, width = integrals.shape
    rows = TILE // 2
    block = pl.BlockSpec((rows, width), lambda i: (i, 0))
    half = jax.ShapeDtypeStruct((depth, width), jnp.bfloat16)
    return pl.pallas_call(
        split_kernel,
        out_shape=(half, half),
        grid=(depth // rows,),
        in_specs=[block],
        out_specs=(block, block),
        compiler_params=pltpu.CompilerParams(vmem_limit_bytes=VMEM_BYTES),
        cost_estimate=pl.CostEstimate(flops=0, bytes_accessed=8 * depth * width, transcendentals=0),
    )(integrals)


def product_kernel(first, ranks, source_ref, flag_ref, *refs):
    amp_refs, (high_ref, low_ref), refs = refs[:ranks], refs[ranks : ranks + 2], refs[ranks + 2 :]
    out_refs, (pair_ref, total_ref) = refs[: 2 * CHAINS], refs[2 * CHAINS :]
    rows = ranks * TILE_ROWS
    width = high_ref.shape[1]
    step = pl.program_id(0)

    @pl.when(step == 0)
    def _():
        for i, amp_ref in enumerate(amp_refs):
            shards, _, wide = amp_ref.shape
            for shard in range(shards):
                value = amp_ref[shard]
                high = value.astype(jnp.bfloat16)
                columns = pl.ds(shard * wide, wide)
                pair_ref[pl.ds(i * TILE_ROWS, TILE_ROWS), columns] = high
                pair_ref[pl.ds(rows + i * TILE_ROWS, TILE_ROWS), columns] = (
                    value - high.astype(jnp.float32)
                ).astype(jnp.bfloat16)

    total_ref[...] = jnp.zeros_like(total_ref)
    for k in range(high_ref.shape[0] // TILE):
        @pl.when(flag_ref[k, (first + step) * width // TILE] != 0)
        def _():
            deep = pl.ds(k * TILE, TILE)
            both = jnp.dot(pair_ref[:, deep], high_ref[deep, :], preferred_element_type=jnp.float32)
            cross = jnp.dot(pair_ref[:rows, deep], low_ref[deep, :], preferred_element_type=jnp.float32)
            total_ref[...] += both[:rows] + (both[rows:] + cross)
    share = width // CHAINS
    for chain, (kept, sent) in enumerate(RANKS):
        columns = pl.ds(chain * share, share)
        for ref, peers in ((out_refs[2 * chain], kept), (out_refs[2 * chain + 1], sent)):
            for i, peer in enumerate(peers):
                ref[i] = total_ref[pl.ds(peer * TILE_ROWS, TILE_ROWS), columns]


def product(r, piece, pieces, ranks, source, int_tiles, gathered, high, low):
    depth, width = high.shape
    shards = depth // gathered.shape[2]
    rows = ranks * TILE_ROWS
    share = COLUMNS // CHAINS
    steps = width // COLUMNS // pieces

    def amp(peer):
        return pl.BlockSpec(
            (shards, TILE_ROWS, depth // shards),
            lambda i, source, flags: (source[r * ranks + peer], 0, 0),
            pipeline_mode=pl.Buffered(1),
        )

    integral = pl.BlockSpec((depth, COLUMNS), lambda i, *_: (0, piece * steps + i))
    return pl.pallas_call(
        functools.partial(product_kernel, piece * steps, ranks),
        out_shape=[jax.ShapeDtypeStruct((2, TILE_ROWS, share * steps), jnp.float32)] * (2 * CHAINS),
        grid_spec=pltpu.PrefetchScalarGridSpec(
            num_scalar_prefetch=2,
            grid=(steps,),
            in_specs=[amp(peer) for peer in range(ranks)] + [integral, integral],
            out_specs=[pl.BlockSpec((2, TILE_ROWS, share), lambda i, *_: (0, 0, i))] * (2 * CHAINS),
            scratch_shapes=[
                pltpu.VMEM((2 * rows, depth), jnp.bfloat16),
                pltpu.VMEM((rows, COLUMNS), jnp.float32),
            ],
        ),
        compiler_params=pltpu.CompilerParams(vmem_limit_bytes=VMEM_BYTES),
        cost_estimate=pl.CostEstimate(
            flops=6 * rows * depth * width // pieces, bytes_accessed=4 * depth * width // pieces, transcendentals=0
        ),
    )(source, int_tiles, *[gathered] * ranks, high, low)


def relay_kernel(*refs):
    for chain in range(CHAINS):
        refs[2 * CHAINS + chain][...] = refs[2 * chain][0] + refs[2 * chain + 1][0]


def relay(kept, heard):
    _, rows, width = kept[0].shape
    passed = pl.BlockSpec((1, rows, width), lambda i: (1, 0, 0))
    out = jax.ShapeDtypeStruct((rows, width), jnp.float32)
    return pl.pallas_call(
        relay_kernel,
        out_shape=[out] * CHAINS,
        grid=(1,),
        in_specs=[passed] * (2 * CHAINS),
        out_specs=[pl.BlockSpec((rows, width), lambda i: (0, 0))] * CHAINS,
    )(*[array for pair in zip(kept, heard) for array in pair])


def finish_kernel(columns, *refs):
    refs = refs[1:]
    parts, (term_ref, denominator_ref), out_ref = refs[: 3 * CHAINS], refs[3 * CHAINS : 3 * CHAINS + 2], refs[-1]
    share = columns // CHAINS
    for block in range(term_ref.shape[1] // columns):
        for chain in range(CHAINS):
            kept, heard, relayed = parts[3 * chain : 3 * chain + 3]
            source = pl.ds(block * share, share)
            target = pl.ds(block * columns + chain * share, share)
            total = kept[0, :, source] + heard[0, :, source] + relayed[:, source]
            out_ref[:, target] = (total + term_ref[:, target]) / denominator_ref[:, target]


def finish(r, piece, slot, kept, heard, relayed, other_terms, denominators, update):
    share = kept[0].shape[2]
    width = share * CHAINS
    first = pl.BlockSpec((1, TILE_ROWS, share), lambda i, slot: (0, 0, 0))
    whole = pl.BlockSpec((TILE_ROWS, share), lambda i, slot: (0, 0))
    owned = pl.BlockSpec((TILE_ROWS, width), lambda i, slot: (slot[r], piece))
    before = [] if update is None else [update]
    return pl.pallas_call(
        functools.partial(finish_kernel, COLUMNS),
        out_shape=jax.ShapeDtypeStruct(other_terms.shape, jnp.float32),
        grid_spec=pltpu.PrefetchScalarGridSpec(
            num_scalar_prefetch=1,
            grid=(1,),
            in_specs=[first, first, whole] * CHAINS
            + [owned, owned]
            + [pl.BlockSpec(memory_space=pl.ANY)] * len(before),
            out_specs=owned,
        ),
        input_output_aliases={3 * CHAINS + 3: 0} if before else {},
        cost_estimate=pl.CostEstimate(flops=0, bytes_accessed=24 * TILE_ROWS * width, transcendentals=0),
    )(
        slot,
        *[array for chain in zip(kept, heard, relayed) for array in chain],
        other_terms,
        denominators,
        *before,
    )


def in_rounds(devices, ranks, amplitudes, amp_tiles, integrals, int_tiles, owner_tiles, other_terms, denominators):
    rank = lax.axis_index("cd").astype(jnp.int32)
    spot = lax.axis_index("ab").astype(jnp.int32)
    tiles = amp_tiles.shape[1]
    half = tiles // CORES

    def gather(array):
        return lax.all_gather(array, "ab", axis=0)

    def swap(sent, peers):
        return [lax.ppermute(array, "cd", [(c, c ^ peer) for c in range(ranks)]) for array, peer in zip(sent, peers)]

    where, source, slot = plan(owner_tiles, jnp.stack([rank, spot]), devices, half)
    whole = take(FIRST, tiles, where, amp_tiles, amplitudes)
    high, low = split(integrals)
    away = take(AWAY, half, where, amp_tiles, amplitudes)
    stay = take(STAY, half, where, amp_tiles, amplitudes)
    came = lax.ppermute(away, "ab", [(i, i ^ 1) for i in range(devices)])
    mine = where[WHOSE] == 0
    shards = [whole, jnp.where(mine, stay, came), jnp.where(mine, came, stay)]
    gathered = [gather(shard) for shard in shards]
    groups = [[(0, 0, 1), (1, 0, 1)], [(2, 0, 1)], [(3, 0, 2), (3, 1, 2)]]
    terms = (other_terms, denominators)
    update, waiting = None, []
    for index, group in enumerate(groups):
        final = index == len(groups) - 1
        if index == 0:
            rows, high, low, *_ = lax.optimization_barrier((gathered[0], high, low, *shards[1:]))
        else:
            rows, onward, update = lax.optimization_barrier((gathered[index], onward, update))
        sums = []
        for r, piece, pieces in group:
            parts = product(r, piece, pieces, ranks, source, int_tiles, rows, high, low)
            if sums:
                parts, heard = lax.optimization_barrier((parts, sums[-1][1]))
                sums[-1] = (sums[-1][0], heard)
            elif waiting:
                parts, relayed = lax.optimization_barrier((parts, [entry[-1] for entry in waiting]))
                waiting = [(*entry[:-1], heard) for entry, heard in zip(waiting, relayed)]
            sums.append((parts[0::2], swap(parts[1::2], (1, 2))))
            if not final:
                for entry in waiting:
                    update = finish(*entry, *terms, update)
                waiting = []
        entries = []
        for (r, piece, _), (kept, heard) in zip(group, sums):
            if final and waiting:
                if entries:
                    for entry in waiting:
                        update = finish(*entry, *terms, update)
                    waiting = []
                    heard, update = lax.optimization_barrier((heard, update))
            onward = relay(kept, heard)
            if final and waiting:
                onward, slot = lax.optimization_barrier((onward, slot))
                waiting = [(*entry[:2], slot, *entry[3:]) for entry in waiting]
            entries.append((r, piece, slot, kept, heard, swap(onward, (2, 1))))
        waiting = entries
    for entry in waiting:
        update = finish(*entry, *terms, update)
    return update


def solution(mesh):
    ranks, places = mesh.shape["cd"], mesh.shape["ab"]

    def on_device(amplitudes, amp_tiles, integrals, int_tiles, owner_tiles, other_terms, denominators):
        args = (amplitudes, amp_tiles, integrals, int_tiles, owner_tiles, other_terms, denominators)
        tiles = owner_tiles.shape[0]
        whole = places % CORES == 0 and amplitudes.shape[1] % (CORES * TILE) == 0
        if whole and ranks == 4 and tiles == 2 * places == ROUNDS * ranks:
            return in_rounds(places, ranks, *args)
        return plain(*args)

    return jax.shard_map(
        on_device,
        mesh=mesh,
        in_specs=(
            P("ab", "cd"),
            P("ab", "cd"),
            P("cd", "ab"),
            P("cd", "ab"),
            P(),
            P("cd", "ab"),
            P("cd", "ab"),
        ),
        out_specs=P("cd", "ab"),
        check_vma=False,
    )
```

```python
import functools

import jax
import jax.numpy as jnp
from jax import lax
from jax.experimental import pallas as pl
from jax.experimental.pallas import tpu as pltpu
from jax.sharding import PartitionSpec as P

TILE = 1024
TILE_ROWS = 128
CORES = 2
VMEM_BYTES = 58 * 1024 * 1024
COLUMNS = 256
ROUNDS = 4
FIRST, AWAY, STAY, WHOSE = 0, 2, 4, 6
CHAINS = 2
RANKS = (((0, 2), (1, 3)), ((0, 1), (2, 3)))


def spread_tiles(tile_flags, row_span, col_span):
    tile_rows, tile_cols = tile_flags.shape
    values = tile_flags.astype(jnp.float32)
    return jnp.broadcast_to(
        values[:, None, :, None], (tile_rows, row_span, tile_cols, col_span)
    ).reshape(tile_rows * row_span, tile_cols * col_span)


def plain(amplitudes, amp_tiles, integrals, int_tiles, owner_tiles, other_terms, denominators):
    masked_ints = integrals * spread_tiles(int_tiles, TILE, TILE)
    masked_amps = amplitudes * spread_tiles(amp_tiles, TILE_ROWS, TILE)
    tile_count = owner_tiles.shape[0]
    gathered = lax.all_gather(masked_amps, "ab", axis=0, tiled=True)
    partial_value = jnp.dot(
        gathered, masked_ints, precision=lax.Precision.HIGHEST, preferred_element_type=jnp.float32
    )
    col_width = partial_value.shape[1]
    partial_value = partial_value.reshape(tile_count, TILE_ROWS, col_width)[owner_tiles].reshape(
        tile_count * TILE_ROWS, col_width
    )
    owned = lax.psum_scatter(partial_value, "cd", scatter_dimension=0, tiled=True)
    return (owned + other_terms) / denominators


def plan_kernel(devices, half, owner_ref, here_ref, take_ref, source_ref, slot_ref, *scratch):
    inverse_ref, color_ref, pair_ref, device_ref, late_ref = scratch
    rank, spot = here_ref[0], here_ref[1]
    ranks = devices * 2 // ROUNDS
    for q in range(2 * devices):
        inverse_ref[owner_ref[q]] = q
        color_ref[q] = -1
    for d in range(devices):
        late_ref[d] = -1

    def walk(first, colors_ref, after):
        def step(state):
            at, _ = state
            colors_ref[at] = 0
            colors_ref[at ^ 1] = 1
            following = after(at ^ 1)
            return following, colors_ref[following]

        lax.while_loop(lambda state: state[1] < 0, step, (jnp.int32(first), colors_ref[first]))

    for t in range(0, 2 * devices, 2):
        walk(t, color_ref, lambda u: owner_ref[inverse_ref[u] ^ 1])
    for c in range(ranks):
        for p in range(2):
            q = ROUNDS * c + 2 * p
            second = color_ref[owner_ref[q]]
            source_ref[p * ranks + (c ^ rank)] = owner_ref[q + second] >> 1
            group = 2 * c + p
            device = owner_ref[q + 1 - second] >> 1
            device_ref[group] = device
            pair_ref[device] = group

            @pl.when(rank == c)
            def _():
                slot_ref[p] = 2 * p + second
                slot_ref[2 + p] = 2 * p + 1 - second

    for d in range(0, devices, 2):
        walk(d, late_ref, lambda u: device_ref[pair_ref[u] ^ 1])
    for c in range(ranks):
        swap = late_ref[device_ref[2 * c]]
        for p in range(2):
            r = 2 + (swap ^ p)
            source_ref[r * ranks + (c ^ rank)] = device_ref[2 * c + p] >> 1

        @pl.when(jnp.logical_and(rank == c, swap != 0))
        def _():
            kept = slot_ref[2]
            slot_ref[2] = slot_ref[3]
            slot_ref[3] = kept

    early = color_ref[2 * spot]
    core = spot % CORES
    take_ref[FIRST] = early
    take_ref[FIRST + 1] = 0
    take_ref[AWAY] = 1 - early
    take_ref[AWAY + 1] = (1 - core) * half
    take_ref[STAY] = 1 - early
    take_ref[STAY + 1] = core * half
    take_ref[WHOSE] = late_ref[spot]


def plan(owner_tiles, here, devices, half):
    tiles = 2 * devices
    smem = pl.BlockSpec(memory_space=pltpu.SMEM)
    ints = jnp.int32
    return pl.pallas_call(
        functools.partial(plan_kernel, devices, half),
        out_shape=(
            jax.ShapeDtypeStruct((WHOSE + 1,), ints),
            jax.ShapeDtypeStruct((tiles,), ints),
            jax.ShapeDtypeStruct((ROUNDS,), ints),
        ),
        in_specs=[smem, smem],
        out_specs=(smem, smem, smem),
        scratch_shapes=[pltpu.SMEM((tiles,), ints)] * 2 + [pltpu.SMEM((devices,), ints)] * 3,
    )(owner_tiles, here)


def take_kernel(at, take_ref, flag_ref, amp_ref, out_ref):
    flag = flag_ref[take_ref[at], take_ref[at + 1] + pl.program_id(0)]
    out_ref[...] = amp_ref[...] * flag.astype(jnp.float32)


def take(at, tiles, where, amp_tiles, amplitudes):
    return pl.pallas_call(
        functools.partial(take_kernel, at),
        out_shape=jax.ShapeDtypeStruct((TILE_ROWS, tiles * TILE), jnp.float32),
        grid_spec=pltpu.PrefetchScalarGridSpec(
            num_scalar_prefetch=2,
            grid=(tiles,),
            in_specs=[
                pl.BlockSpec((TILE_ROWS, TILE), lambda j, where, flags: (where[at], where[at + 1] + j))
            ],
            out_specs=pl.BlockSpec((TILE_ROWS, TILE), lambda j, where, flags: (0, j)),
        ),
    )(where, amp_tiles, amplitudes)


def split_kernel(value_ref, halves_ref):
    value = value_ref[...]
    high = value.astype(jnp.bfloat16)
    halves_ref[:TILE, :] = high
    halves_ref[TILE:, :] = (value - high.astype(jnp.float32)).astype(jnp.bfloat16)


def split(integrals):
    depth, width = integrals.shape
    return pl.pallas_call(
        split_kernel,
        out_shape=jax.ShapeDtypeStruct((2 * depth, width), jnp.bfloat16),
        grid=(depth // TILE, width // TILE),
        in_specs=[pl.BlockSpec((TILE, TILE), lambda i, j: (i, j))],
        out_specs=pl.BlockSpec((2 * TILE, TILE), lambda i, j: (i, j)),
        compiler_params=pltpu.CompilerParams(vmem_limit_bytes=VMEM_BYTES),
        cost_estimate=pl.CostEstimate(flops=0, bytes_accessed=8 * depth * width, transcendentals=0),
    )(integrals)


def product_kernel(first, ranks, source_ref, flag_ref, *refs):
    amp_refs, halves_ref, refs = refs[:ranks], refs[ranks], refs[ranks + 1 :]
    out_refs, (twice_ref, low_ref, total_ref) = refs[: 2 * CHAINS], refs[2 * CHAINS :]
    width = halves_ref.shape[1]
    step = pl.program_id(0)

    @pl.when(step == 0)
    def _():
        for i, amp_ref in enumerate(amp_refs):
            rows = pl.ds(i * TILE_ROWS, TILE_ROWS)
            shards, _, wide = amp_ref.shape
            for shard in range(shards):
                for tile in range(wide // TILE):
                    k = shard * (wide // TILE) + tile
                    value = amp_ref[shard, :, pl.ds(tile * TILE, TILE)]
                    high = value.astype(jnp.bfloat16)
                    twice_ref[rows, pl.ds(2 * k * TILE, TILE)] = high
                    twice_ref[rows, pl.ds((2 * k + 1) * TILE, TILE)] = high
                    low_ref[rows, pl.ds(k * TILE, TILE)] = (value - high.astype(jnp.float32)).astype(jnp.bfloat16)

    total_ref[...] = jnp.zeros_like(total_ref)
    for k in range(low_ref.shape[1] // TILE):
        @pl.when(flag_ref[k, (first + step) * width // TILE] != 0)
        def _():
            total = total_ref[...]
            total = total + jnp.dot(
                low_ref[:, pl.ds(k * TILE, TILE)],
                halves_ref[pl.ds(2 * k * TILE, TILE), :],
                preferred_element_type=jnp.float32,
            )
            deep = pl.ds(2 * k * TILE, 2 * TILE)
            total_ref[...] = total + jnp.dot(
                twice_ref[:, deep], halves_ref[deep, :], preferred_element_type=jnp.float32
            )
    share = width // CHAINS
    for chain, (kept, sent) in enumerate(RANKS):
        columns = pl.ds(chain * share, share)
        for ref, peers in ((out_refs[2 * chain], kept), (out_refs[2 * chain + 1], sent)):
            for i, peer in enumerate(peers):
                ref[i] = total_ref[pl.ds(peer * TILE_ROWS, TILE_ROWS), columns]


def product(r, piece, pieces, ranks, source, int_tiles, gathered, halves):
    depth, width = halves.shape[0] // 2, halves.shape[1]
    shards = depth // gathered.shape[2]
    rows = ranks * TILE_ROWS
    share = COLUMNS // CHAINS
    steps = width // COLUMNS // pieces

    def amp(peer):
        return pl.BlockSpec(
            (shards, TILE_ROWS, depth // shards),
            lambda i, source, flags: (source[r * ranks + peer], 0, 0),
            pipeline_mode=pl.Buffered(1),
        )

    integral = pl.BlockSpec((2 * depth, COLUMNS), lambda i, *_: (0, piece * steps + i))
    return pl.pallas_call(
        functools.partial(product_kernel, piece * steps, ranks),
        out_shape=[jax.ShapeDtypeStruct((2, TILE_ROWS, share * steps), jnp.float32)] * (2 * CHAINS),
        grid_spec=pltpu.PrefetchScalarGridSpec(
            num_scalar_prefetch=2,
            grid=(steps,),
            in_specs=[amp(peer) for peer in range(ranks)] + [integral],
            out_specs=[pl.BlockSpec((2, TILE_ROWS, share), lambda i, *_: (0, 0, i))] * (2 * CHAINS),
            scratch_shapes=[
                pltpu.VMEM((rows, 2 * depth), jnp.bfloat16),
                pltpu.VMEM((rows, depth), jnp.bfloat16),
                pltpu.VMEM((rows, COLUMNS), jnp.float32),
            ],
        ),
        compiler_params=pltpu.CompilerParams(vmem_limit_bytes=VMEM_BYTES),
        cost_estimate=pl.CostEstimate(
            flops=6 * rows * depth * width // pieces, bytes_accessed=4 * depth * width // pieces, transcendentals=0
        ),
    )(source, int_tiles, *[gathered] * ranks, halves)


def relay_kernel(*refs):
    for chain in range(CHAINS):
        refs[2 * CHAINS + chain][...] = refs[2 * chain][0] + refs[2 * chain + 1][0]


def relay(kept, heard):
    _, rows, width = kept[0].shape
    passed = pl.BlockSpec((1, rows, width), lambda i: (1, 0, 0))
    out = jax.ShapeDtypeStruct((rows, width), jnp.float32)
    return pl.pallas_call(
        relay_kernel,
        out_shape=[out] * CHAINS,
        grid=(1,),
        in_specs=[passed] * (2 * CHAINS),
        out_specs=[pl.BlockSpec((rows, width), lambda i: (0, 0))] * CHAINS,
    )(*[array for pair in zip(kept, heard) for array in pair])


def finish_kernel(columns, *refs):
    refs = refs[1:]
    parts, (term_ref, denominator_ref), out_ref = refs[: 3 * CHAINS], refs[3 * CHAINS : 3 * CHAINS + 2], refs[-1]
    share = columns // CHAINS
    for block in range(term_ref.shape[1] // columns):
        for chain in range(CHAINS):
            kept, heard, relayed = parts[3 * chain : 3 * chain + 3]
            source = pl.ds(block * share, share)
            target = pl.ds(block * columns + chain * share, share)
            total = kept[0, :, source] + heard[0, :, source] + relayed[:, source]
            out_ref[:, target] = (total + term_ref[:, target]) / denominator_ref[:, target]


def finish(r, piece, slot, kept, heard, relayed, other_terms, denominators, update):
    share = kept[0].shape[2]
    width = share * CHAINS
    first = pl.BlockSpec((1, TILE_ROWS, share), lambda i, slot: (0, 0, 0))
    whole = pl.BlockSpec((TILE_ROWS, share), lambda i, slot: (0, 0))
    owned = pl.BlockSpec((TILE_ROWS, width), lambda i, slot: (slot[r], piece))
    before = [] if update is None else [update]
    return pl.pallas_call(
        functools.partial(finish_kernel, COLUMNS),
        out_shape=jax.ShapeDtypeStruct(other_terms.shape, jnp.float32),
        grid_spec=pltpu.PrefetchScalarGridSpec(
            num_scalar_prefetch=1,
            grid=(1,),
            in_specs=[first, first, whole] * CHAINS
            + [owned, owned]
            + [pl.BlockSpec(memory_space=pl.ANY)] * len(before),
            out_specs=owned,
        ),
        input_output_aliases={3 * CHAINS + 3: 0} if before else {},
        cost_estimate=pl.CostEstimate(flops=0, bytes_accessed=24 * TILE_ROWS * width, transcendentals=0),
    )(
        slot,
        *[array for chain in zip(kept, heard, relayed) for array in chain],
        other_terms,
        denominators,
        *before,
    )


def in_rounds(devices, ranks, amplitudes, amp_tiles, integrals, int_tiles, owner_tiles, other_terms, denominators):
    rank = lax.axis_index("cd").astype(jnp.int32)
    spot = lax.axis_index("ab").astype(jnp.int32)
    tiles = amp_tiles.shape[1]
    half = tiles // CORES

    def gather(array):
        return lax.all_gather(array, "ab", axis=0)

    def swap(sent, peers):
        return [lax.ppermute(array, "cd", [(c, c ^ peer) for c in range(ranks)]) for array, peer in zip(sent, peers)]

    where, source, slot = plan(owner_tiles, jnp.stack([rank, spot]), devices, half)
    whole = take(FIRST, tiles, where, amp_tiles, amplitudes)
    halves = split(integrals)
    away = take(AWAY, half, where, amp_tiles, amplitudes)
    stay = take(STAY, half, where, amp_tiles, amplitudes)
    came = lax.ppermute(away, "ab", [(i, i ^ 1) for i in range(devices)])
    mine = where[WHOSE] == 0
    shards = [whole, jnp.where(mine, stay, came), jnp.where(mine, came, stay)]
    gathered = [gather(shard) for shard in shards]
    groups = [[(0, 0, 1), (1, 0, 1)], [(2, 0, 1)], [(3, 0, 2), (3, 1, 2)]]
    terms = (other_terms, denominators)
    update, waiting = None, []
    for index, group in enumerate(groups):
        final = index == len(groups) - 1
        if index == 0:
            rows, halves, *_ = lax.optimization_barrier((gathered[0], halves, *shards[1:]))
        else:
            if final:
                for entry in waiting:
                    update = finish(*entry, *terms, update)
                waiting = []
            rows, onward, update = lax.optimization_barrier((gathered[index], onward, update))
        sums = []
        for r, piece, pieces in group:
            parts = product(r, piece, pieces, ranks, source, int_tiles, rows, halves)
            if sums:
                parts, heard = lax.optimization_barrier((parts, sums[-1][1]))
                sums[-1] = (sums[-1][0], heard)
            elif waiting:
                parts, relayed = lax.optimization_barrier((parts, [entry[-1] for entry in waiting]))
                waiting = [(*entry[:-1], heard) for entry, heard in zip(waiting, relayed)]
            sums.append((parts[0::2], swap(parts[1::2], (1, 2))))
            for entry in waiting:
                update = finish(*entry, *terms, update)
            waiting = []
        entries = []
        for (r, piece, _), (kept, heard) in zip(group, sums):
            onward = relay(kept, heard)
            entries.append((r, piece, slot, kept, heard, swap(onward, (2, 1))))
        waiting = entries
    for entry in waiting:
        update = finish(*entry, *terms, update)
    return update


def solution(mesh):
    ranks, places = mesh.shape["cd"], mesh.shape["ab"]

    def on_device(amplitudes, amp_tiles, integrals, int_tiles, owner_tiles, other_terms, denominators):
        args = (amplitudes, amp_tiles, integrals, int_tiles, owner_tiles, other_terms, denominators)
        tiles = owner_tiles.shape[0]
        whole = places % CORES == 0 and amplitudes.shape[1] % (CORES * TILE) == 0
        if whole and ranks == 4 and tiles == 2 * places == ROUNDS * ranks:
            return in_rounds(places, ranks, *args)
        return plain(*args)

    return jax.shard_map(
        on_device,
        mesh=mesh,
        in_specs=(
            P("ab", "cd"),
            P("ab", "cd"),
            P("cd", "ab"),
            P("cd", "ab"),
            P(),
            P("cd", "ab"),
            P("cd", "ab"),
        ),
        out_specs=P("cd", "ab"),
        check_vma=False,
    )
```

```python
import functools

import jax
import jax.numpy as jnp
from jax import lax
from jax.experimental import pallas as pl
from jax.experimental.pallas import tpu as pltpu
from jax.sharding import PartitionSpec as P

TILE = 1024
TILE_ROWS = 128
CORES = 2
VMEM_BYTES = 58 * 1024 * 1024
COLUMNS = 256
ROUNDS = 4
FIRST, AWAY, STAY, WHOSE = 0, 2, 4, 6
CHAINS = 2
RANKS = (((0, 2), (1, 3)), ((0, 1), (2, 3)))


def spread_tiles(tile_flags, row_span, col_span):
    tile_rows, tile_cols = tile_flags.shape
    values = tile_flags.astype(jnp.float32)
    return jnp.broadcast_to(
        values[:, None, :, None], (tile_rows, row_span, tile_cols, col_span)
    ).reshape(tile_rows * row_span, tile_cols * col_span)


def plain(amplitudes, amp_tiles, integrals, int_tiles, owner_tiles, other_terms, denominators):
    masked_ints = integrals * spread_tiles(int_tiles, TILE, TILE)
    masked_amps = amplitudes * spread_tiles(amp_tiles, TILE_ROWS, TILE)
    tile_count = owner_tiles.shape[0]
    gathered = lax.all_gather(masked_amps, "ab", axis=0, tiled=True)
    partial_value = jnp.dot(
        gathered, masked_ints, precision=lax.Precision.HIGHEST, preferred_element_type=jnp.float32
    )
    col_width = partial_value.shape[1]
    partial_value = partial_value.reshape(tile_count, TILE_ROWS, col_width)[owner_tiles].reshape(
        tile_count * TILE_ROWS, col_width
    )
    owned = lax.psum_scatter(partial_value, "cd", scatter_dimension=0, tiled=True)
    return (owned + other_terms) / denominators


def plan_kernel(devices, half, owner_ref, here_ref, take_ref, source_ref, slot_ref, *scratch):
    inverse_ref, color_ref, pair_ref, device_ref, late_ref = scratch
    rank, spot = here_ref[0], here_ref[1]
    ranks = devices * 2 // ROUNDS
    for q in range(2 * devices):
        inverse_ref[owner_ref[q]] = q
        color_ref[q] = -1
    for d in range(devices):
        late_ref[d] = -1

    def walk(first, colors_ref, after):
        def step(state):
            at, _ = state
            colors_ref[at] = 0
            colors_ref[at ^ 1] = 1
            following = after(at ^ 1)
            return following, colors_ref[following]

        lax.while_loop(lambda state: state[1] < 0, step, (jnp.int32(first), colors_ref[first]))

    for t in range(0, 2 * devices, 2):
        walk(t, color_ref, lambda u: owner_ref[inverse_ref[u] ^ 1])
    for c in range(ranks):
        for p in range(2):
            q = ROUNDS * c + 2 * p
            second = color_ref[owner_ref[q]]
            source_ref[p * ranks + (c ^ rank)] = owner_ref[q + second] >> 1
            group = 2 * c + p
            device = owner_ref[q + 1 - second] >> 1
            device_ref[group] = device
            pair_ref[device] = group

            @pl.when(rank == c)
            def _():
                slot_ref[p] = 2 * p + second
                slot_ref[2 + p] = 2 * p + 1 - second

    for d in range(0, devices, 2):
        walk(d, late_ref, lambda u: device_ref[pair_ref[u] ^ 1])
    for c in range(ranks):
        swap = late_ref[device_ref[2 * c]]
        for p in range(2):
            r = 2 + (swap ^ p)
            source_ref[r * ranks + (c ^ rank)] = device_ref[2 * c + p] >> 1

        @pl.when(jnp.logical_and(rank == c, swap != 0))
        def _():
            kept = slot_ref[2]
            slot_ref[2] = slot_ref[3]
            slot_ref[3] = kept

    early = color_ref[2 * spot]
    core = spot % CORES
    take_ref[FIRST] = early
    take_ref[FIRST + 1] = 0
    take_ref[AWAY] = 1 - early
    take_ref[AWAY + 1] = (1 - core) * half
    take_ref[STAY] = 1 - early
    take_ref[STAY + 1] = core * half
    take_ref[WHOSE] = late_ref[spot]


def plan(owner_tiles, here, devices, half):
    tiles = 2 * devices
    smem = pl.BlockSpec(memory_space=pltpu.SMEM)
    ints = jnp.int32
    return pl.pallas_call(
        functools.partial(plan_kernel, devices, half),
        out_shape=(
            jax.ShapeDtypeStruct((WHOSE + 1,), ints),
            jax.ShapeDtypeStruct((tiles,), ints),
            jax.ShapeDtypeStruct((ROUNDS,), ints),
        ),
        in_specs=[smem, smem],
        out_specs=(smem, smem, smem),
        scratch_shapes=[pltpu.SMEM((tiles,), ints)] * 2 + [pltpu.SMEM((devices,), ints)] * 3,
    )(owner_tiles, here)


def take_kernel(at, take_ref, flag_ref, amp_ref, out_ref):
    flag = flag_ref[take_ref[at], take_ref[at + 1] + pl.program_id(0)]
    out_ref[...] = amp_ref[...] * flag.astype(jnp.float32)


def take(at, tiles, where, amp_tiles, amplitudes):
    return pl.pallas_call(
        functools.partial(take_kernel, at),
        out_shape=jax.ShapeDtypeStruct((TILE_ROWS, tiles * TILE), jnp.float32),
        grid_spec=pltpu.PrefetchScalarGridSpec(
            num_scalar_prefetch=2,
            grid=(tiles,),
            in_specs=[
                pl.BlockSpec((TILE_ROWS, TILE), lambda j, where, flags: (where[at], where[at + 1] + j))
            ],
            out_specs=pl.BlockSpec((TILE_ROWS, TILE), lambda j, where, flags: (0, j)),
        ),
    )(where, amp_tiles, amplitudes)


def split_kernel(value_ref, halves_ref):
    value = value_ref[...]
    high = value.astype(jnp.bfloat16)
    halves_ref[:TILE, :] = high
    halves_ref[TILE:, :] = (value - high.astype(jnp.float32)).astype(jnp.bfloat16)


def split(integrals):
    depth, width = integrals.shape
    return pl.pallas_call(
        split_kernel,
        out_shape=jax.ShapeDtypeStruct((2 * depth, width), jnp.bfloat16),
        grid=(depth // TILE, width // TILE),
        in_specs=[pl.BlockSpec((TILE, TILE), lambda i, j: (i, j))],
        out_specs=pl.BlockSpec((2 * TILE, TILE), lambda i, j: (i, j)),
        compiler_params=pltpu.CompilerParams(vmem_limit_bytes=VMEM_BYTES),
        cost_estimate=pl.CostEstimate(flops=0, bytes_accessed=8 * depth * width, transcendentals=0),
    )(integrals)


def product_kernel(first, ranks, source_ref, flag_ref, *refs):
    amp_refs, halves_ref, refs = refs[:ranks], refs[ranks], refs[ranks + 1 :]
    out_refs, (twice_ref, low_ref, total_ref) = refs[: 2 * CHAINS], refs[2 * CHAINS :]
    width = halves_ref.shape[1]
    step = pl.program_id(0)

    @pl.when(step == 0)
    def _():
        for i, amp_ref in enumerate(amp_refs):
            rows = pl.ds(i * TILE_ROWS, TILE_ROWS)
            shards, _, wide = amp_ref.shape
            for shard in range(shards):
                for tile in range(wide // TILE):
                    k = shard * (wide // TILE) + tile
                    value = amp_ref[shard, :, pl.ds(tile * TILE, TILE)]
                    high = value.astype(jnp.bfloat16)
                    twice_ref[rows, pl.ds(2 * k * TILE, TILE)] = high
                    twice_ref[rows, pl.ds((2 * k + 1) * TILE, TILE)] = high
                    low_ref[rows, pl.ds(k * TILE, TILE)] = (value - high.astype(jnp.float32)).astype(jnp.bfloat16)

    total_ref[...] = jnp.zeros_like(total_ref)
    for k in range(low_ref.shape[1] // TILE):
        @pl.when(flag_ref[k, (first + step) * width // TILE] != 0)
        def _():
            total = total_ref[...]
            total = total + jnp.dot(
                low_ref[:, pl.ds(k * TILE, TILE)],
                halves_ref[pl.ds(2 * k * TILE, TILE), :],
                preferred_element_type=jnp.float32,
            )
            deep = pl.ds(2 * k * TILE, 2 * TILE)
            total_ref[...] = total + jnp.dot(
                twice_ref[:, deep], halves_ref[deep, :], preferred_element_type=jnp.float32
            )
    share = width // CHAINS
    for chain, (kept, sent) in enumerate(RANKS):
        columns = pl.ds(chain * share, share)
        for ref, peers in ((out_refs[2 * chain], kept), (out_refs[2 * chain + 1], sent)):
            for i, peer in enumerate(peers):
                ref[i] = total_ref[pl.ds(peer * TILE_ROWS, TILE_ROWS), columns]


def product(r, first, steps, ranks, source, int_tiles, gathered, halves):
    depth, width = halves.shape[0] // 2, halves.shape[1]
    shards = depth // gathered.shape[2]
    rows = ranks * TILE_ROWS
    share = COLUMNS // CHAINS

    def amp(peer):
        return pl.BlockSpec(
            (shards, TILE_ROWS, depth // shards),
            lambda i, source, flags: (source[r * ranks + peer], 0, 0),
            pipeline_mode=pl.Buffered(1),
        )

    integral = pl.BlockSpec((2 * depth, COLUMNS), lambda i, *_: (0, first + i))
    return pl.pallas_call(
        functools.partial(product_kernel, first, ranks),
        out_shape=[jax.ShapeDtypeStruct((2, TILE_ROWS, share * steps), jnp.float32)] * (2 * CHAINS),
        grid_spec=pltpu.PrefetchScalarGridSpec(
            num_scalar_prefetch=2,
            grid=(steps,),
            in_specs=[amp(peer) for peer in range(ranks)] + [integral],
            out_specs=[pl.BlockSpec((2, TILE_ROWS, share), lambda i, *_: (0, 0, i))] * (2 * CHAINS),
            scratch_shapes=[
                pltpu.VMEM((rows, 2 * depth), jnp.bfloat16),
                pltpu.VMEM((rows, depth), jnp.bfloat16),
                pltpu.VMEM((rows, COLUMNS), jnp.float32),
            ],
        ),
        compiler_params=pltpu.CompilerParams(vmem_limit_bytes=VMEM_BYTES),
        cost_estimate=pl.CostEstimate(
            flops=6 * rows * depth * steps * COLUMNS, bytes_accessed=4 * depth * steps * COLUMNS, transcendentals=0
        ),
    )(source, int_tiles, *[gathered] * ranks, halves)


def relay_kernel(*refs):
    for chain in range(CHAINS):
        refs[2 * CHAINS + chain][...] = refs[2 * chain][0] + refs[2 * chain + 1][0]


def relay(kept, heard):
    _, rows, width = kept[0].shape
    passed = pl.BlockSpec((1, rows, width), lambda i: (1, 0, 0))
    out = jax.ShapeDtypeStruct((rows, width), jnp.float32)
    return pl.pallas_call(
        relay_kernel,
        out_shape=[out] * CHAINS,
        grid=(1,),
        in_specs=[passed] * (2 * CHAINS),
        out_specs=[pl.BlockSpec((rows, width), lambda i: (0, 0))] * CHAINS,
    )(*[array for pair in zip(kept, heard) for array in pair])


def finish_kernel(columns, *refs):
    refs = refs[1:]
    parts, (term_ref, denominator_ref), out_ref = refs[: 3 * CHAINS], refs[3 * CHAINS : 3 * CHAINS + 2], refs[-1]
    share = columns // CHAINS
    for block in range(term_ref.shape[1] // columns):
        for chain in range(CHAINS):
            kept, heard, relayed = parts[3 * chain : 3 * chain + 3]
            source = pl.ds(block * share, share)
            target = pl.ds(block * columns + chain * share, share)
            total = kept[0, :, source] + heard[0, :, source] + relayed[:, source]
            out_ref[:, target] = (total + term_ref[:, target]) / denominator_ref[:, target]


def finish(r, start, slot, kept, heard, relayed, other_terms, denominators, update):
    share = kept[0].shape[2]
    width = share * CHAINS
    first = pl.BlockSpec((1, TILE_ROWS, share), lambda i, slot: (0, 0, 0))
    whole = pl.BlockSpec((TILE_ROWS, share), lambda i, slot: (0, 0))
    owned = pl.BlockSpec((TILE_ROWS, width), lambda i, slot: (slot[r], start * COLUMNS // width))
    before = [] if update is None else [update]
    return pl.pallas_call(
        functools.partial(finish_kernel, COLUMNS),
        out_shape=jax.ShapeDtypeStruct(other_terms.shape, jnp.float32),
        grid_spec=pltpu.PrefetchScalarGridSpec(
            num_scalar_prefetch=1,
            grid=(1,),
            in_specs=[first, first, whole] * CHAINS
            + [owned, owned]
            + [pl.BlockSpec(memory_space=pl.ANY)] * len(before),
            out_specs=owned,
        ),
        input_output_aliases={3 * CHAINS + 3: 0} if before else {},
        cost_estimate=pl.CostEstimate(flops=0, bytes_accessed=24 * TILE_ROWS * width, transcendentals=0),
    )(
        slot,
        *[array for chain in zip(kept, heard, relayed) for array in chain],
        other_terms,
        denominators,
        *before,
    )


def in_rounds(devices, ranks, amplitudes, amp_tiles, integrals, int_tiles, owner_tiles, other_terms, denominators):
    rank = lax.axis_index("cd").astype(jnp.int32)
    spot = lax.axis_index("ab").astype(jnp.int32)
    tiles = amp_tiles.shape[1]
    half = tiles // CORES

    def gather(array):
        return lax.all_gather(array, "ab", axis=0)

    def swap(sent, peers):
        return [lax.ppermute(array, "cd", [(c, c ^ peer) for c in range(ranks)]) for array, peer in zip(sent, peers)]

    where, source, slot = plan(owner_tiles, jnp.stack([rank, spot]), devices, half)
    whole = take(FIRST, tiles, where, amp_tiles, amplitudes)
    halves = split(integrals)
    away = take(AWAY, half, where, amp_tiles, amplitudes)
    stay = take(STAY, half, where, amp_tiles, amplitudes)
    came = lax.ppermute(away, "ab", [(i, i ^ 1) for i in range(devices)])
    mine = where[WHOSE] == 0
    shards = [whole, jnp.where(mine, stay, came), jnp.where(mine, came, stay)]
    gathered = [gather(shard) for shard in shards]
    terms = (other_terms, denominators)
    tie = lax.optimization_barrier
    steps = halves.shape[1] // COLUMNS
    most = steps * 3 // 4

    def begin(r, rows, first=0, count=steps):
        return product(r, first, count, ranks, source, int_tiles, rows, halves)

    def send(parts):
        return swap(parts[1::2], (1, 2))

    def pass_on(parts, heard):
        onward = relay(parts[0::2], heard)
        return onward, swap(onward, (2, 1))

    rows, halves, *_ = tie((gathered[0], halves, *shards[1:]))
    parts0 = begin(0, rows)
    heard0 = send(parts0)
    parts1, heard0 = tie((begin(1, rows), heard0))
    heard1 = send(parts1)
    onward, relayed0 = pass_on(parts0, heard0)

    rows, onward = tie((gathered[1], onward))
    parts2, relayed0, heard1 = tie((begin(2, rows), relayed0, heard1))
    heard2 = send(parts2)
    onward, relayed1 = pass_on(parts1, heard1)
    slot, onward = tie((slot, onward))
    update = finish(0, 0, slot, parts0[0::2], heard0, relayed0, *terms, None)
    heard2, update = tie((heard2, update))
    onward, relayed2 = pass_on(parts2, heard2)
    update = finish(1, 0, slot, parts1[0::2], heard1, relayed1, *terms, update)

    rows, onward, update = tie((gathered[2], onward, update))
    parts3, relayed2 = tie((begin(3, rows, 0, most), relayed2))
    heard3 = send(parts3)
    parts4, heard3 = tie((begin(3, rows, most, steps - most), heard3))
    heard4 = send(parts4)
    onward, relayed3 = pass_on(parts3, heard3)
    slot, onward = tie((slot, onward))
    update = finish(2, 0, slot, parts2[0::2], heard2, relayed2, *terms, update)
    heard4, update = tie((heard4, update))
    _, relayed4 = pass_on(parts4, heard4)
    update = finish(3, 0, slot, parts3[0::2], heard3, relayed3, *terms, update)
    return finish(3, most, slot, parts4[0::2], heard4, relayed4, *terms, update)


def solution(mesh):
    ranks, places = mesh.shape["cd"], mesh.shape["ab"]

    def on_device(amplitudes, amp_tiles, integrals, int_tiles, owner_tiles, other_terms, denominators):
        args = (amplitudes, amp_tiles, integrals, int_tiles, owner_tiles, other_terms, denominators)
        tiles = owner_tiles.shape[0]
        whole = places % CORES == 0 and amplitudes.shape[1] % (CORES * TILE) == 0
        if whole and ranks == 4 and tiles == 2 * places == ROUNDS * ranks:
            return in_rounds(places, ranks, *args)
        return plain(*args)

    return jax.shard_map(
        on_device,
        mesh=mesh,
        in_specs=(
            P("ab", "cd"),
            P("ab", "cd"),
            P("cd", "ab"),
            P("cd", "ab"),
            P(),
            P("cd", "ab"),
            P("cd", "ab"),
        ),
        out_specs=P("cd", "ab"),
        check_vma=False,
    )
```

```python
import functools

import jax
import jax.numpy as jnp
from jax import lax
from jax.experimental import pallas as pl
from jax.experimental.pallas import tpu as pltpu
from jax.sharding import PartitionSpec as P

TILE = 1024
TILE_ROWS = 128
CORES = 2
VMEM_BYTES = 58 * 1024 * 1024
COLUMNS = 256
ROUNDS = 4
FIRST, AWAY, STAY, WHOSE = 0, 2, 4, 6
CHAINS = 2
RANKS = (((0, 2), (1, 3)), ((0, 1), (2, 3)))


def spread_tiles(tile_flags, row_span, col_span):
    tile_rows, tile_cols = tile_flags.shape
    values = tile_flags.astype(jnp.float32)
    return jnp.broadcast_to(
        values[:, None, :, None], (tile_rows, row_span, tile_cols, col_span)
    ).reshape(tile_rows * row_span, tile_cols * col_span)


def plain(amplitudes, amp_tiles, integrals, int_tiles, owner_tiles, other_terms, denominators):
    masked_ints = integrals * spread_tiles(int_tiles, TILE, TILE)
    masked_amps = amplitudes * spread_tiles(amp_tiles, TILE_ROWS, TILE)
    tile_count = owner_tiles.shape[0]
    gathered = lax.all_gather(masked_amps, "ab", axis=0, tiled=True)
    partial_value = jnp.dot(
        gathered, masked_ints, precision=lax.Precision.HIGHEST, preferred_element_type=jnp.float32
    )
    col_width = partial_value.shape[1]
    partial_value = partial_value.reshape(tile_count, TILE_ROWS, col_width)[owner_tiles].reshape(
        tile_count * TILE_ROWS, col_width
    )
    owned = lax.psum_scatter(partial_value, "cd", scatter_dimension=0, tiled=True)
    return (owned + other_terms) / denominators


def plan_kernel(devices, half, owner_ref, here_ref, take_ref, source_ref, slot_ref, *scratch):
    inverse_ref, color_ref, pair_ref, device_ref, late_ref = scratch
    rank, spot = here_ref[0], here_ref[1]
    ranks = devices * 2 // ROUNDS
    for q in range(2 * devices):
        inverse_ref[owner_ref[q]] = q
        color_ref[q] = -1
    for d in range(devices):
        late_ref[d] = -1

    def walk(first, colors_ref, after):
        def step(state):
            at, _ = state
            colors_ref[at] = 0
            colors_ref[at ^ 1] = 1
            following = after(at ^ 1)
            return following, colors_ref[following]

        lax.while_loop(lambda state: state[1] < 0, step, (jnp.int32(first), colors_ref[first]))

    for t in range(0, 2 * devices, 2):
        walk(t, color_ref, lambda u: owner_ref[inverse_ref[u] ^ 1])
    for c in range(ranks):
        for p in range(2):
            q = ROUNDS * c + 2 * p
            second = color_ref[owner_ref[q]]
            source_ref[p * ranks + (c ^ rank)] = owner_ref[q + second] >> 1
            group = 2 * c + p
            device = owner_ref[q + 1 - second] >> 1
            device_ref[group] = device
            pair_ref[device] = group

            @pl.when(rank == c)
            def _():
                slot_ref[p] = 2 * p + second
                slot_ref[2 + p] = 2 * p + 1 - second

    for d in range(0, devices, 2):
        walk(d, late_ref, lambda u: device_ref[pair_ref[u] ^ 1])
    for c in range(ranks):
        swap = late_ref[device_ref[2 * c]]
        for p in range(2):
            r = 2 + (swap ^ p)
            source_ref[r * ranks + (c ^ rank)] = device_ref[2 * c + p] >> 1

        @pl.when(jnp.logical_and(rank == c, swap != 0))
        def _():
            kept = slot_ref[2]
            slot_ref[2] = slot_ref[3]
            slot_ref[3] = kept

    early = color_ref[2 * spot]
    core = spot % CORES
    take_ref[FIRST] = early
    take_ref[FIRST + 1] = 0
    take_ref[AWAY] = 1 - early
    take_ref[AWAY + 1] = (1 - core) * half
    take_ref[STAY] = 1 - early
    take_ref[STAY + 1] = core * half
    take_ref[WHOSE] = late_ref[spot]


def plan(owner_tiles, here, devices, half):
    tiles = 2 * devices
    smem = pl.BlockSpec(memory_space=pltpu.SMEM)
    ints = jnp.int32
    return pl.pallas_call(
        functools.partial(plan_kernel, devices, half),
        out_shape=(
            jax.ShapeDtypeStruct((WHOSE + 1,), ints),
            jax.ShapeDtypeStruct((tiles,), ints),
            jax.ShapeDtypeStruct((ROUNDS,), ints),
        ),
        in_specs=[smem, smem],
        out_specs=(smem, smem, smem),
        scratch_shapes=[pltpu.SMEM((tiles,), ints)] * 2 + [pltpu.SMEM((devices,), ints)] * 3,
    )(owner_tiles, here)


def take_kernel(at, take_ref, flag_ref, amp_ref, out_ref):
    flag = flag_ref[take_ref[at], take_ref[at + 1] + pl.program_id(0)]
    out_ref[...] = amp_ref[...] * flag.astype(jnp.float32)


def take(at, tiles, where, amp_tiles, amplitudes):
    return pl.pallas_call(
        functools.partial(take_kernel, at),
        out_shape=jax.ShapeDtypeStruct((TILE_ROWS, tiles * TILE), jnp.float32),
        grid_spec=pltpu.PrefetchScalarGridSpec(
            num_scalar_prefetch=2,
            grid=(tiles,),
            in_specs=[
                pl.BlockSpec((TILE_ROWS, TILE), lambda j, where, flags: (where[at], where[at + 1] + j))
            ],
            out_specs=pl.BlockSpec((TILE_ROWS, TILE), lambda j, where, flags: (0, j)),
        ),
    )(where, amp_tiles, amplitudes)


def split_kernel(value_ref, halves_ref):
    value = value_ref[...]
    high = value.astype(jnp.bfloat16)
    halves_ref[:TILE, :] = high
    halves_ref[TILE:, :] = (value - high.astype(jnp.float32)).astype(jnp.bfloat16)


def split(integrals):
    depth, width = integrals.shape
    return pl.pallas_call(
        split_kernel,
        out_shape=jax.ShapeDtypeStruct((2 * depth, width), jnp.bfloat16),
        grid=(depth // TILE, width // TILE),
        in_specs=[pl.BlockSpec((TILE, TILE), lambda i, j: (i, j))],
        out_specs=pl.BlockSpec((2 * TILE, TILE), lambda i, j: (i, j)),
        compiler_params=pltpu.CompilerParams(vmem_limit_bytes=VMEM_BYTES),
        cost_estimate=pl.CostEstimate(flops=0, bytes_accessed=8 * depth * width, transcendentals=0),
    )(integrals)


def product_kernel(r, first, ranks, source_ref, flag_ref, *refs):
    amp_ref, halves_ref, refs = refs[0], refs[1], refs[2:]
    out_refs, (tiles_ref, twice_ref, low_ref, total_ref, ready) = refs[: 2 * CHAINS], refs[2 * CHAINS :]
    width = halves_ref.shape[1]
    step = pl.program_id(0)

    @pl.when(step == 0)
    def _():
        shards, _, wide = tiles_ref.shape[1:]
        copies = []
        for i in range(ranks):
            shard = pl.ds(source_ref[r * ranks + i] * shards, shards)
            copies.append(pltpu.make_async_copy(amp_ref.at[shard], tiles_ref.at[i], ready.at[i]))
            copies[i].start()
        for i in range(ranks):
            copies[i].wait()
            rows = pl.ds(i * TILE_ROWS, TILE_ROWS)
            for shard in range(shards):
                for tile in range(wide // TILE):
                    k = shard * (wide // TILE) + tile
                    value = tiles_ref[i, shard, :, pl.ds(tile * TILE, TILE)]
                    high = value.astype(jnp.bfloat16)
                    twice_ref[rows, pl.ds(2 * k * TILE, TILE)] = high
                    twice_ref[rows, pl.ds((2 * k + 1) * TILE, TILE)] = high
                    low_ref[rows, pl.ds(k * TILE, TILE)] = (value - high.astype(jnp.float32)).astype(jnp.bfloat16)

    total_ref[...] = jnp.zeros_like(total_ref)
    for k in range(low_ref.shape[1] // TILE):
        @pl.when(flag_ref[k, (first + step) * width // TILE] != 0)
        def _():
            total = total_ref[...]
            total = total + jnp.dot(
                low_ref[:, pl.ds(k * TILE, TILE)],
                halves_ref[pl.ds(2 * k * TILE, TILE), :],
                preferred_element_type=jnp.float32,
            )
            deep = pl.ds(2 * k * TILE, 2 * TILE)
            total_ref[...] = total + jnp.dot(
                twice_ref[:, deep], halves_ref[deep, :], preferred_element_type=jnp.float32
            )
    share = width // CHAINS
    for chain, (kept, sent) in enumerate(RANKS):
        columns = pl.ds(chain * share, share)
        for ref, peers in ((out_refs[2 * chain], kept), (out_refs[2 * chain + 1], sent)):
            for i, peer in enumerate(peers):
                ref[i] = total_ref[pl.ds(peer * TILE_ROWS, TILE_ROWS), columns]


def product(r, first, steps, ranks, source, int_tiles, gathered, halves):
    depth, width = halves.shape[0] // 2, halves.shape[1]
    shards = depth // gathered.shape[2]
    rows = ranks * TILE_ROWS
    share = COLUMNS // CHAINS

    integral = pl.BlockSpec((2 * depth, COLUMNS), lambda i, *_: (0, first + i))
    return pl.pallas_call(
        functools.partial(product_kernel, r, first, ranks),
        out_shape=[jax.ShapeDtypeStruct((2, TILE_ROWS, share * steps), jnp.float32)] * (2 * CHAINS),
        grid_spec=pltpu.PrefetchScalarGridSpec(
            num_scalar_prefetch=2,
            grid=(steps,),
            in_specs=[pl.BlockSpec(memory_space=pl.ANY), integral],
            out_specs=[pl.BlockSpec((2, TILE_ROWS, share), lambda i, *_: (0, 0, i))] * (2 * CHAINS),
            scratch_shapes=[
                pltpu.VMEM((ranks, shards, TILE_ROWS, depth // shards), jnp.float32),
                pltpu.VMEM((rows, 2 * depth), jnp.bfloat16),
                pltpu.VMEM((rows, depth), jnp.bfloat16),
                pltpu.VMEM((rows, COLUMNS), jnp.float32),
                pltpu.SemaphoreType.DMA((ranks,)),
            ],
        ),
        compiler_params=pltpu.CompilerParams(vmem_limit_bytes=VMEM_BYTES),
        cost_estimate=pl.CostEstimate(
            flops=6 * rows * depth * steps * COLUMNS, bytes_accessed=4 * depth * steps * COLUMNS, transcendentals=0
        ),
    )(source, int_tiles, gathered, halves)


def relay_kernel(*refs):
    for chain in range(CHAINS):
        refs[2 * CHAINS + chain][...] = refs[2 * chain][0] + refs[2 * chain + 1][0]


def relay(kept, heard):
    _, rows, width = kept[0].shape
    passed = pl.BlockSpec((1, rows, width), lambda i: (1, 0, 0))
    out = jax.ShapeDtypeStruct((rows, width), jnp.float32)
    return pl.pallas_call(
        relay_kernel,
        out_shape=[out] * CHAINS,
        grid=(1,),
        in_specs=[passed] * (2 * CHAINS),
        out_specs=[pl.BlockSpec((rows, width), lambda i: (0, 0))] * CHAINS,
    )(*[array for pair in zip(kept, heard) for array in pair])


def finish_kernel(columns, *refs):
    refs = refs[1:]
    parts, (term_ref, denominator_ref), out_ref = refs[: 3 * CHAINS], refs[3 * CHAINS : 3 * CHAINS + 2], refs[-1]
    share = columns // CHAINS
    for block in range(term_ref.shape[1] // columns):
        for chain in range(CHAINS):
            kept, heard, relayed = parts[3 * chain : 3 * chain + 3]
            source = pl.ds(block * share, share)
            target = pl.ds(block * columns + chain * share, share)
            total = kept[0, :, source] + heard[0, :, source] + relayed[:, source]
            out_ref[:, target] = (total + term_ref[:, target]) / denominator_ref[:, target]


def finish(r, start, slot, kept, heard, relayed, other_terms, denominators, update):
    blocks = 2 if start == 0 else 1
    share = kept[0].shape[2] // blocks
    width = share * CHAINS
    first = pl.BlockSpec((1, TILE_ROWS, share), lambda i, slot: (0, 0, i))
    whole = pl.BlockSpec((TILE_ROWS, share), lambda i, slot: (0, i))
    owned = pl.BlockSpec((TILE_ROWS, width), lambda i, slot: (slot[r], start * COLUMNS // width + i))
    before = [] if update is None else [update]
    return pl.pallas_call(
        functools.partial(finish_kernel, COLUMNS),
        out_shape=jax.ShapeDtypeStruct(other_terms.shape, jnp.float32),
        grid_spec=pltpu.PrefetchScalarGridSpec(
            num_scalar_prefetch=1,
            grid=(blocks,),
            in_specs=[first, first, whole] * CHAINS
            + [owned, owned]
            + [pl.BlockSpec(memory_space=pl.ANY)] * len(before),
            out_specs=owned,
        ),
        input_output_aliases={3 * CHAINS + 3: 0} if before else {},
        cost_estimate=pl.CostEstimate(flops=0, bytes_accessed=24 * TILE_ROWS * width, transcendentals=0),
    )(
        slot,
        *[array for chain in zip(kept, heard, relayed) for array in chain],
        other_terms,
        denominators,
        *before,
    )


def in_rounds(devices, ranks, amplitudes, amp_tiles, integrals, int_tiles, owner_tiles, other_terms, denominators):
    rank = lax.axis_index("cd").astype(jnp.int32)
    spot = lax.axis_index("ab").astype(jnp.int32)
    tiles = amp_tiles.shape[1]
    half = tiles // CORES

    def gather(array):
        return lax.all_gather(array, "ab", axis=0)

    def swap(sent, peers):
        return [lax.ppermute(array, "cd", [(c, c ^ peer) for c in range(ranks)]) for array, peer in zip(sent, peers)]

    where, source, slot = plan(owner_tiles, jnp.stack([rank, spot]), devices, half)
    whole = take(FIRST, tiles, where, amp_tiles, amplitudes)
    halves = split(integrals)
    away = take(AWAY, half, where, amp_tiles, amplitudes)
    stay = take(STAY, half, where, amp_tiles, amplitudes)
    came = lax.ppermute(away, "ab", [(i, i ^ 1) for i in range(devices)])
    mine = where[WHOSE] == 0
    shards = [whole, jnp.where(mine, stay, came), jnp.where(mine, came, stay)]
    gathered = [gather(shard) for shard in shards]
    terms = (other_terms, denominators)
    tie = lax.optimization_barrier
    steps = halves.shape[1] // COLUMNS
    most = steps * 3 // 4

    def begin(r, rows, first=0, count=steps):
        return product(r, first, count, ranks, source, int_tiles, rows, halves)

    def send(parts):
        return swap(parts[1::2], (1, 2))

    def pass_on(parts, heard):
        onward = relay(parts[0::2], heard)
        return onward, swap(onward, (2, 1))

    rows, halves, *_ = tie((gathered[0], halves, *shards[1:]))
    parts0 = begin(0, rows)
    heard0 = send(parts0)
    parts1, heard0 = tie((begin(1, rows), heard0))
    heard1 = send(parts1)
    onward, relayed0 = pass_on(parts0, heard0)

    rows, onward = tie((gathered[1], onward))
    parts2, relayed0, heard1 = tie((begin(2, rows), relayed0, heard1))
    onward, relayed1 = pass_on(parts1, heard1)
    parts2, slot, onward = tie((parts2, slot, onward))
    heard2 = send(parts2)
    update = finish(0, 0, slot, parts0[0::2], heard0, relayed0, *terms, None)
    update = finish(1, 0, slot, parts1[0::2], heard1, relayed1, *terms, update)
    heard2, update = tie((heard2, update))
    onward, relayed2 = pass_on(parts2, heard2)

    rows, onward, update = tie((gathered[2], onward, update))
    parts3, relayed2 = tie((begin(3, rows, 0, most), relayed2))
    heard3 = send(parts3)
    parts4, heard3 = tie((begin(3, rows, most, steps - most), heard3))
    heard4 = send(parts4)
    onward, relayed3 = pass_on(parts3, heard3)
    slot, onward = tie((slot, onward))
    update = finish(2, 0, slot, parts2[0::2], heard2, relayed2, *terms, update)
    heard4, update = tie((heard4, update))
    _, relayed4 = pass_on(parts4, heard4)
    update = finish(3, 0, slot, parts3[0::2], heard3, relayed3, *terms, update)
    return finish(3, most, slot, parts4[0::2], heard4, relayed4, *terms, update)


def solution(mesh):
    ranks, places = mesh.shape["cd"], mesh.shape["ab"]

    def on_device(amplitudes, amp_tiles, integrals, int_tiles, owner_tiles, other_terms, denominators):
        args = (amplitudes, amp_tiles, integrals, int_tiles, owner_tiles, other_terms, denominators)
        tiles = owner_tiles.shape[0]
        whole = places % CORES == 0 and amplitudes.shape[1] % (CORES * TILE) == 0
        if whole and ranks == 4 and tiles == 2 * places == ROUNDS * ranks:
            return in_rounds(places, ranks, *args)
        return plain(*args)

    return jax.shard_map(
        on_device,
        mesh=mesh,
        in_specs=(
            P("ab", "cd"),
            P("ab", "cd"),
            P("cd", "ab"),
            P("cd", "ab"),
            P(),
            P("cd", "ab"),
            P("cd", "ab"),
        ),
        out_specs=P("cd", "ab"),
        check_vma=False,
    )
```

```python
import functools

import jax
import jax.numpy as jnp
from jax import lax
from jax.experimental import pallas as pl
from jax.experimental.pallas import tpu as pltpu
from jax.sharding import PartitionSpec as P

TILE = 1024
TILE_ROWS = 128
CORES = 2
VMEM_BYTES = 58 * 1024 * 1024
COLUMNS = 256
ROUNDS = 4
FIRST, AWAY, STAY, WHOSE = 0, 2, 4, 6
CHAINS = 2
RANKS = (((0, 2), (1, 3)), ((0, 1), (2, 3)))


def spread_tiles(tile_flags, row_span, col_span):
    tile_rows, tile_cols = tile_flags.shape
    values = tile_flags.astype(jnp.float32)
    return jnp.broadcast_to(
        values[:, None, :, None], (tile_rows, row_span, tile_cols, col_span)
    ).reshape(tile_rows * row_span, tile_cols * col_span)


def plain(amplitudes, amp_tiles, integrals, int_tiles, owner_tiles, other_terms, denominators):
    masked_ints = integrals * spread_tiles(int_tiles, TILE, TILE)
    masked_amps = amplitudes * spread_tiles(amp_tiles, TILE_ROWS, TILE)
    tile_count = owner_tiles.shape[0]
    gathered = lax.all_gather(masked_amps, "ab", axis=0, tiled=True)
    partial_value = jnp.dot(
        gathered, masked_ints, precision=lax.Precision.HIGHEST, preferred_element_type=jnp.float32
    )
    col_width = partial_value.shape[1]
    partial_value = partial_value.reshape(tile_count, TILE_ROWS, col_width)[owner_tiles].reshape(
        tile_count * TILE_ROWS, col_width
    )
    owned = lax.psum_scatter(partial_value, "cd", scatter_dimension=0, tiled=True)
    return (owned + other_terms) / denominators


def plan_kernel(devices, half, owner_ref, here_ref, take_ref, source_ref, slot_ref, tile_ref, *scratch):
    inverse_ref, color_ref, pair_ref, device_ref, late_ref = scratch
    rank, spot = here_ref[0], here_ref[1]
    ranks = devices * 2 // ROUNDS
    for q in range(2 * devices):
        inverse_ref[owner_ref[q]] = q
        color_ref[q] = -1
    for d in range(devices):
        late_ref[d] = -1

    def walk(first, colors_ref, after):
        def step(state):
            at, _ = state
            colors_ref[at] = 0
            colors_ref[at ^ 1] = 1
            following = after(at ^ 1)
            return following, colors_ref[following]

        lax.while_loop(lambda state: state[1] < 0, step, (jnp.int32(first), colors_ref[first]))

    for t in range(0, 2 * devices, 2):
        walk(t, color_ref, lambda u: owner_ref[inverse_ref[u] ^ 1])
    for c in range(ranks):
        for p in range(2):
            q = ROUNDS * c + 2 * p
            second = color_ref[owner_ref[q]]
            source_ref[p * ranks + (c ^ rank)] = owner_ref[q + second] >> 1
            tile_ref[p * ranks + (c ^ rank)] = owner_ref[q + second]
            group = 2 * c + p
            device = owner_ref[q + 1 - second] >> 1
            device_ref[group] = device
            pair_ref[device] = group

            @pl.when(rank == c)
            def _():
                slot_ref[p] = 2 * p + second
                slot_ref[2 + p] = 2 * p + 1 - second

    for d in range(0, devices, 2):
        walk(d, late_ref, lambda u: device_ref[pair_ref[u] ^ 1])
    for c in range(ranks):
        swap = late_ref[device_ref[2 * c]]
        for p in range(2):
            r = 2 + (swap ^ p)
            device = device_ref[2 * c + p]
            source_ref[r * ranks + (c ^ rank)] = device >> 1
            tile_ref[r * ranks + (c ^ rank)] = 2 * device + 1 - color_ref[2 * device]

        @pl.when(jnp.logical_and(rank == c, swap != 0))
        def _():
            kept = slot_ref[2]
            slot_ref[2] = slot_ref[3]
            slot_ref[3] = kept

    early = color_ref[2 * spot]
    core = spot % CORES
    take_ref[FIRST] = early
    take_ref[FIRST + 1] = 0
    take_ref[AWAY] = 1 - early
    take_ref[AWAY + 1] = (1 - core) * half
    take_ref[STAY] = 1 - early
    take_ref[STAY + 1] = core * half
    take_ref[WHOSE] = late_ref[spot]


def plan(owner_tiles, here, devices, half):
    tiles = 2 * devices
    smem = pl.BlockSpec(memory_space=pltpu.SMEM)
    ints = jnp.int32
    return pl.pallas_call(
        functools.partial(plan_kernel, devices, half),
        out_shape=(
            jax.ShapeDtypeStruct((WHOSE + 1,), ints),
            jax.ShapeDtypeStruct((tiles,), ints),
            jax.ShapeDtypeStruct((ROUNDS,), ints),
            jax.ShapeDtypeStruct((tiles,), ints),
        ),
        in_specs=[smem, smem],
        out_specs=(smem, smem, smem, smem),
        scratch_shapes=[pltpu.SMEM((tiles,), ints)] * 2 + [pltpu.SMEM((devices,), ints)] * 3,
    )(owner_tiles, here)


def take_kernel(at, take_ref, flag_ref, amp_ref, out_ref):
    flag = flag_ref[take_ref[at], take_ref[at + 1] + pl.program_id(0)]
    out_ref[...] = amp_ref[...] * flag.astype(jnp.float32)


def take(at, tiles, where, amp_tiles, amplitudes):
    return pl.pallas_call(
        functools.partial(take_kernel, at),
        out_shape=jax.ShapeDtypeStruct((TILE_ROWS, tiles * TILE), jnp.float32),
        grid_spec=pltpu.PrefetchScalarGridSpec(
            num_scalar_prefetch=2,
            grid=(tiles,),
            in_specs=[
                pl.BlockSpec((TILE_ROWS, TILE), lambda j, where, flags: (where[at], where[at + 1] + j))
            ],
            out_specs=pl.BlockSpec((TILE_ROWS, TILE), lambda j, where, flags: (0, j)),
        ),
    )(where, amp_tiles, amplitudes)


def split_kernel(value_ref, halves_ref):
    value = value_ref[...]
    high = value.astype(jnp.bfloat16)
    halves_ref[:TILE, :] = high
    halves_ref[TILE:, :] = (value - high.astype(jnp.float32)).astype(jnp.bfloat16)


def split(integrals):
    depth, width = integrals.shape
    return pl.pallas_call(
        split_kernel,
        out_shape=jax.ShapeDtypeStruct((2 * depth, width), jnp.bfloat16),
        grid=(depth // TILE, width // TILE),
        in_specs=[pl.BlockSpec((TILE, TILE), lambda i, j: (i, j))],
        out_specs=pl.BlockSpec((2 * TILE, TILE), lambda i, j: (i, j)),
        compiler_params=pltpu.CompilerParams(vmem_limit_bytes=VMEM_BYTES),
        cost_estimate=pl.CostEstimate(flops=0, bytes_accessed=8 * depth * width, transcendentals=0),
    )(integrals)


def product_kernel(r, first, ranks, source_ref, tile_ref, row_flag_ref, flag_ref, amp_ref, halves_ref, *refs):
    out_refs, (tiles_ref, twice_ref, low_ref, total_ref, count_ref, row_ref, ready) = (
        refs[: 2 * CHAINS],
        refs[2 * CHAINS :],
    )
    width = halves_ref.shape[1]
    depth = low_ref.shape[1] // TILE
    step = pl.program_id(0)

    @pl.when(step == 0)
    def _():
        shards, _, wide = tiles_ref.shape[1:]
        copies = []
        for i in range(ranks):
            shard = pl.ds(source_ref[r * ranks + i] * shards, shards)
            copies.append(pltpu.make_async_copy(amp_ref.at[shard], tiles_ref.at[i], ready.at[i]))
            copies[i].start()
        for k in range(depth):
            count_ref[k] = 0
        for i in range(ranks):
            copies[i].wait()
            for shard in range(shards):
                for tile in range(wide // TILE):
                    k = shard * (wide // TILE) + tile

                    @pl.when(row_flag_ref[tile_ref[r * ranks + i], k] != 0)
                    def _():
                        count = count_ref[k]
                        row_ref[k * ranks + count] = i
                        count_ref[k] = count + 1
                        rows = pl.ds(pl.multiple_of(count * TILE_ROWS, TILE_ROWS), TILE_ROWS)
                        value = tiles_ref[i, shard, :, pl.ds(tile * TILE, TILE)]
                        high = value.astype(jnp.bfloat16)
                        twice_ref[rows, pl.ds(2 * k * TILE, TILE)] = high
                        twice_ref[rows, pl.ds((2 * k + 1) * TILE, TILE)] = high
                        low_ref[rows, pl.ds(k * TILE, TILE)] = (value - high.astype(jnp.float32)).astype(
                            jnp.bfloat16
                        )

    total_ref[...] = jnp.zeros_like(total_ref)
    for k in range(depth):
        needed = flag_ref[k, (first + step) * width // TILE] != 0
        for count in range(1, ranks + 1):

            @pl.when(jnp.logical_and(needed, count_ref[k] == count))
            def _():
                rows = pl.ds(0, count * TILE_ROWS)
                deep = pl.ds(2 * k * TILE, 2 * TILE)
                part = jnp.dot(
                    low_ref[rows, pl.ds(k * TILE, TILE)],
                    halves_ref[pl.ds(2 * k * TILE, TILE), :],
                    preferred_element_type=jnp.float32,
                )
                part = part + jnp.dot(
                    twice_ref[rows, deep], halves_ref[deep, :], preferred_element_type=jnp.float32
                )
                for j in range(count):
                    at = pl.ds(pl.multiple_of(row_ref[k * ranks + j] * TILE_ROWS, TILE_ROWS), TILE_ROWS)
                    total_ref[at, :] += part[j * TILE_ROWS : (j + 1) * TILE_ROWS]

    share = width // CHAINS
    for chain, (kept, sent) in enumerate(RANKS):
        columns = pl.ds(chain * share, share)
        for ref, peers in ((out_refs[2 * chain], kept), (out_refs[2 * chain + 1], sent)):
            for i, peer in enumerate(peers):
                ref[i] = total_ref[pl.ds(peer * TILE_ROWS, TILE_ROWS), columns]


def product(r, first, steps, ranks, source, tile, row_flags, int_tiles, gathered, halves):
    depth, width = halves.shape[0] // 2, halves.shape[1]
    shards = depth // gathered.shape[2]
    rows = ranks * TILE_ROWS
    share = COLUMNS // CHAINS

    integral = pl.BlockSpec((2 * depth, COLUMNS), lambda i, *_: (0, first + i))
    return pl.pallas_call(
        functools.partial(product_kernel, r, first, ranks),
        out_shape=[jax.ShapeDtypeStruct((2, TILE_ROWS, share * steps), jnp.float32)] * (2 * CHAINS),
        grid_spec=pltpu.PrefetchScalarGridSpec(
            num_scalar_prefetch=4,
            grid=(steps,),
            in_specs=[pl.BlockSpec(memory_space=pl.ANY), integral],
            out_specs=[pl.BlockSpec((2, TILE_ROWS, share), lambda i, *_: (0, 0, i))] * (2 * CHAINS),
            scratch_shapes=[
                pltpu.VMEM((ranks, shards, TILE_ROWS, depth // shards), jnp.float32),
                pltpu.VMEM((rows, 2 * depth), jnp.bfloat16),
                pltpu.VMEM((rows, depth), jnp.bfloat16),
                pltpu.VMEM((rows, COLUMNS), jnp.float32),
                pltpu.SMEM((depth // TILE,), jnp.int32),
                pltpu.SMEM((depth // TILE * ranks,), jnp.int32),
                pltpu.SemaphoreType.DMA((ranks,)),
            ],
        ),
        compiler_params=pltpu.CompilerParams(vmem_limit_bytes=VMEM_BYTES),
        cost_estimate=pl.CostEstimate(
            flops=6 * rows * depth * steps * COLUMNS, bytes_accessed=4 * depth * steps * COLUMNS, transcendentals=0
        ),
    )(source, tile, row_flags, int_tiles, gathered, halves)


def relay_kernel(*refs):
    for chain in range(CHAINS):
        refs[2 * CHAINS + chain][...] = refs[2 * chain][0] + refs[2 * chain + 1][0]


def relay(kept, heard):
    _, rows, width = kept[0].shape
    passed = pl.BlockSpec((1, rows, width), lambda i: (1, 0, 0))
    out = jax.ShapeDtypeStruct((rows, width), jnp.float32)
    return pl.pallas_call(
        relay_kernel,
        out_shape=[out] * CHAINS,
        grid=(1,),
        in_specs=[passed] * (2 * CHAINS),
        out_specs=[pl.BlockSpec((rows, width), lambda i: (0, 0))] * CHAINS,
    )(*[array for pair in zip(kept, heard) for array in pair])


def finish_kernel(columns, *refs):
    refs = refs[1:]
    parts, (term_ref, denominator_ref), out_ref = refs[: 3 * CHAINS], refs[3 * CHAINS : 3 * CHAINS + 2], refs[-1]
    share = columns // CHAINS
    for block in range(term_ref.shape[1] // columns):
        for chain in range(CHAINS):
            kept, heard, relayed = parts[3 * chain : 3 * chain + 3]
            source = pl.ds(block * share, share)
            target = pl.ds(block * columns + chain * share, share)
            total = kept[0, :, source] + heard[0, :, source] + relayed[:, source]
            out_ref[:, target] = (total + term_ref[:, target]) / denominator_ref[:, target]


def finish(r, start, slot, kept, heard, relayed, other_terms, denominators, update):
    blocks = 2 if start == 0 else 1
    share = kept[0].shape[2] // blocks
    width = share * CHAINS
    first = pl.BlockSpec((1, TILE_ROWS, share), lambda i, slot: (0, 0, i))
    whole = pl.BlockSpec((TILE_ROWS, share), lambda i, slot: (0, i))
    owned = pl.BlockSpec((TILE_ROWS, width), lambda i, slot: (slot[r], start * COLUMNS // width + i))
    before = [] if update is None else [update]
    return pl.pallas_call(
        functools.partial(finish_kernel, COLUMNS),
        out_shape=jax.ShapeDtypeStruct(other_terms.shape, jnp.float32),
        grid_spec=pltpu.PrefetchScalarGridSpec(
            num_scalar_prefetch=1,
            grid=(blocks,),
            in_specs=[first, first, whole] * CHAINS
            + [owned, owned]
            + [pl.BlockSpec(memory_space=pl.ANY)] * len(before),
            out_specs=owned,
        ),
        input_output_aliases={3 * CHAINS + 3: 0} if before else {},
        cost_estimate=pl.CostEstimate(flops=0, bytes_accessed=24 * TILE_ROWS * width, transcendentals=0),
    )(
        slot,
        *[array for chain in zip(kept, heard, relayed) for array in chain],
        other_terms,
        denominators,
        *before,
    )


def in_rounds(devices, ranks, amplitudes, amp_tiles, integrals, int_tiles, owner_tiles, other_terms, denominators):
    rank = lax.axis_index("cd").astype(jnp.int32)
    spot = lax.axis_index("ab").astype(jnp.int32)
    tiles = amp_tiles.shape[1]
    half = tiles // CORES

    def gather(array):
        return lax.all_gather(array, "ab", axis=0)

    def swap(sent, peers):
        return [lax.ppermute(array, "cd", [(c, c ^ peer) for c in range(ranks)]) for array, peer in zip(sent, peers)]

    where, source, slot, tile = plan(owner_tiles, jnp.stack([rank, spot]), devices, half)
    whole = take(FIRST, tiles, where, amp_tiles, amplitudes)
    halves = split(integrals)
    away = take(AWAY, half, where, amp_tiles, amplitudes)
    stay = take(STAY, half, where, amp_tiles, amplitudes)
    came = lax.ppermute(away, "ab", [(i, i ^ 1) for i in range(devices)])
    mine = where[WHOSE] == 0
    shards = [whole, jnp.where(mine, stay, came), jnp.where(mine, came, stay)]
    gathered = [gather(shard) for shard in shards]
    terms = (other_terms, denominators)
    tie = lax.optimization_barrier
    steps = halves.shape[1] // COLUMNS
    most = steps * 3 // 4

    def begin(r, rows, first=0, count=steps):
        return product(r, first, count, ranks, source, tile, row_flags, int_tiles, rows, halves)

    def send(parts):
        return swap(parts[1::2], (1, 2))

    def pass_on(parts, heard):
        onward = relay(parts[0::2], heard)
        return onward, swap(onward, (2, 1))

    row_flags, halves = tie((amp_tiles, halves))
    for bit in range((devices - 1).bit_length()):
        reach = 1 << bit
        came = lax.ppermute(row_flags, "ab", [(i, i ^ reach) for i in range(devices)])
        row_flags = jnp.where(
            spot & reach == 0, jnp.concatenate([row_flags, came]), jnp.concatenate([came, row_flags])
        )
    rows, halves, row_flags, *_ = tie((gathered[0], halves, row_flags, *shards[1:]))
    parts0 = begin(0, rows)
    heard0 = send(parts0)
    parts1, heard0 = tie((begin(1, rows), heard0))
    heard1 = send(parts1)
    onward, relayed0 = pass_on(parts0, heard0)

    rows, onward = tie((gathered[1], onward))
    parts2, relayed0, heard1 = tie((begin(2, rows), relayed0, heard1))
    onward, relayed1 = pass_on(parts1, heard1)
    parts2, slot, onward = tie((parts2, slot, onward))
    heard2 = send(parts2)
    update = finish(0, 0, slot, parts0[0::2], heard0, relayed0, *terms, None)
    update = finish(1, 0, slot, parts1[0::2], heard1, relayed1, *terms, update)
    heard2, update = tie((heard2, update))
    onward, relayed2 = pass_on(parts2, heard2)

    rows, onward, update = tie((gathered[2], onward, update))
    parts3, relayed2 = tie((begin(3, rows, 0, most), relayed2))
    heard3 = send(parts3)
    parts4, heard3 = tie((begin(3, rows, most, steps - most), heard3))
    heard4 = send(parts4)
    onward, relayed3 = pass_on(parts3, heard3)
    slot, onward = tie((slot, onward))
    update = finish(2, 0, slot, parts2[0::2], heard2, relayed2, *terms, update)
    heard4, update = tie((heard4, update))
    _, relayed4 = pass_on(parts4, heard4)
    update = finish(3, 0, slot, parts3[0::2], heard3, relayed3, *terms, update)
    return finish(3, most, slot, parts4[0::2], heard4, relayed4, *terms, update)


def solution(mesh):
    ranks, places = mesh.shape["cd"], mesh.shape["ab"]

    def on_device(amplitudes, amp_tiles, integrals, int_tiles, owner_tiles, other_terms, denominators):
        args = (amplitudes, amp_tiles, integrals, int_tiles, owner_tiles, other_terms, denominators)
        tiles = owner_tiles.shape[0]
        whole = places % CORES == 0 and amplitudes.shape[1] % (CORES * TILE) == 0
        if whole and ranks == 4 and tiles == 2 * places == ROUNDS * ranks:
            return in_rounds(places, ranks, *args)
        return plain(*args)

    return jax.shard_map(
        on_device,
        mesh=mesh,
        in_specs=(
            P("ab", "cd"),
            P("ab", "cd"),
            P("cd", "ab"),
            P("cd", "ab"),
            P(),
            P("cd", "ab"),
            P("cd", "ab"),
        ),
        out_specs=P("cd", "ab"),
        check_vma=False,
    )
```

```python
import functools

import jax
import jax.numpy as jnp
from jax import lax
from jax.experimental import pallas as pl
from jax.experimental.pallas import tpu as pltpu
from jax.sharding import PartitionSpec as P

TILE = 1024
TILE_ROWS = 128
CORES = 2
VMEM_BYTES = 58 * 1024 * 1024
COLUMNS = 256
ROUNDS = 4
FIRST, AWAY, STAY, WHOSE = 0, 2, 4, 6
CHAINS = 2
RANKS = (((0, 2), (1, 3)), ((0, 1), (2, 3)))


def spread_tiles(tile_flags, row_span, col_span):
    tile_rows, tile_cols = tile_flags.shape
    values = tile_flags.astype(jnp.float32)
    return jnp.broadcast_to(
        values[:, None, :, None], (tile_rows, row_span, tile_cols, col_span)
    ).reshape(tile_rows * row_span, tile_cols * col_span)


def plain(amplitudes, amp_tiles, integrals, int_tiles, owner_tiles, other_terms, denominators):
    masked_ints = integrals * spread_tiles(int_tiles, TILE, TILE)
    masked_amps = amplitudes * spread_tiles(amp_tiles, TILE_ROWS, TILE)
    tile_count = owner_tiles.shape[0]
    gathered = lax.all_gather(masked_amps, "ab", axis=0, tiled=True)
    partial_value = jnp.dot(
        gathered, masked_ints, precision=lax.Precision.HIGHEST, preferred_element_type=jnp.float32
    )
    col_width = partial_value.shape[1]
    partial_value = partial_value.reshape(tile_count, TILE_ROWS, col_width)[owner_tiles].reshape(
        tile_count * TILE_ROWS, col_width
    )
    owned = lax.psum_scatter(partial_value, "cd", scatter_dimension=0, tiled=True)
    return (owned + other_terms) / denominators


def plan_kernel(devices, half, owner_ref, here_ref, take_ref, source_ref, slot_ref, tile_ref, *scratch):
    inverse_ref, color_ref, pair_ref, device_ref, late_ref = scratch
    rank, spot = here_ref[0], here_ref[1]
    ranks = devices * 2 // ROUNDS
    for q in range(2 * devices):
        inverse_ref[owner_ref[q]] = q
        color_ref[q] = -1
    for d in range(devices):
        late_ref[d] = -1

    def walk(first, colors_ref, after):
        def step(state):
            at, _ = state
            colors_ref[at] = 0
            colors_ref[at ^ 1] = 1
            following = after(at ^ 1)
            return following, colors_ref[following]

        lax.while_loop(lambda state: state[1] < 0, step, (jnp.int32(first), colors_ref[first]))

    for t in range(0, 2 * devices, 2):
        walk(t, color_ref, lambda u: owner_ref[inverse_ref[u] ^ 1])
    for c in range(ranks):
        for p in range(2):
            q = ROUNDS * c + 2 * p
            second = color_ref[owner_ref[q]]
            source_ref[p * ranks + (c ^ rank)] = owner_ref[q + second] >> 1
            tile_ref[p * ranks + (c ^ rank)] = owner_ref[q + second]
            group = 2 * c + p
            device = owner_ref[q + 1 - second] >> 1
            device_ref[group] = device
            pair_ref[device] = group

            @pl.when(rank == c)
            def _():
                slot_ref[p] = 2 * p + second
                slot_ref[2 + p] = 2 * p + 1 - second

    for d in range(0, devices, 2):
        walk(d, late_ref, lambda u: device_ref[pair_ref[u] ^ 1])
    for c in range(ranks):
        swap = late_ref[device_ref[2 * c]]
        for p in range(2):
            r = 2 + (swap ^ p)
            device = device_ref[2 * c + p]
            source_ref[r * ranks + (c ^ rank)] = device >> 1
            tile_ref[r * ranks + (c ^ rank)] = 2 * device + 1 - color_ref[2 * device]

        @pl.when(jnp.logical_and(rank == c, swap != 0))
        def _():
            kept = slot_ref[2]
            slot_ref[2] = slot_ref[3]
            slot_ref[3] = kept

    early = color_ref[2 * spot]
    core = spot % CORES
    take_ref[FIRST] = early
    take_ref[FIRST + 1] = 0
    take_ref[AWAY] = 1 - early
    take_ref[AWAY + 1] = (1 - core) * half
    take_ref[STAY] = 1 - early
    take_ref[STAY + 1] = core * half
    take_ref[WHOSE] = late_ref[spot]


def plan(owner_tiles, here, devices, half):
    tiles = 2 * devices
    smem = pl.BlockSpec(memory_space=pltpu.SMEM)
    ints = jnp.int32
    return pl.pallas_call(
        functools.partial(plan_kernel, devices, half),
        out_shape=(
            jax.ShapeDtypeStruct((WHOSE + 1,), ints),
            jax.ShapeDtypeStruct((tiles,), ints),
            jax.ShapeDtypeStruct((ROUNDS,), ints),
            jax.ShapeDtypeStruct((tiles,), ints),
        ),
        in_specs=[smem, smem],
        out_specs=(smem, smem, smem, smem),
        scratch_shapes=[pltpu.SMEM((tiles,), ints)] * 2 + [pltpu.SMEM((devices,), ints)] * 3,
    )(owner_tiles, here)


def take_kernel(at, take_ref, flag_ref, amp_ref, out_ref):
    flag = flag_ref[take_ref[at], take_ref[at + 1] + pl.program_id(0)]
    out_ref[...] = amp_ref[...] * flag.astype(jnp.float32)


def take(at, tiles, where, amp_tiles, amplitudes):
    return pl.pallas_call(
        functools.partial(take_kernel, at),
        out_shape=jax.ShapeDtypeStruct((TILE_ROWS, tiles * TILE), jnp.float32),
        grid_spec=pltpu.PrefetchScalarGridSpec(
            num_scalar_prefetch=2,
            grid=(tiles,),
            in_specs=[
                pl.BlockSpec((TILE_ROWS, TILE), lambda j, where, flags: (where[at], where[at + 1] + j))
            ],
            out_specs=pl.BlockSpec((TILE_ROWS, TILE), lambda j, where, flags: (0, j)),
        ),
    )(where, amp_tiles, amplitudes)


def split_kernel(value_ref, halves_ref):
    value = value_ref[...]
    high = value.astype(jnp.bfloat16)
    halves_ref[:TILE, :] = high
    halves_ref[TILE:, :] = (value - high.astype(jnp.float32)).astype(jnp.bfloat16)


def split(integrals):
    depth, width = integrals.shape
    return pl.pallas_call(
        split_kernel,
        out_shape=jax.ShapeDtypeStruct((2 * depth, width), jnp.bfloat16),
        grid=(depth // TILE, width // TILE),
        in_specs=[pl.BlockSpec((TILE, TILE), lambda i, j: (i, j))],
        out_specs=pl.BlockSpec((2 * TILE, TILE), lambda i, j: (i, j)),
        compiler_params=pltpu.CompilerParams(vmem_limit_bytes=VMEM_BYTES),
        cost_estimate=pl.CostEstimate(flops=0, bytes_accessed=8 * depth * width, transcendentals=0),
    )(integrals)


def product_kernel(r, first, ranks, source_ref, tile_ref, row_flag_ref, flag_ref, amp_ref, halves_ref, *refs):
    out_refs, (tiles_ref, twice_ref, low_ref, total_ref, count_ref, row_ref, ready) = (
        refs[: 2 * CHAINS],
        refs[2 * CHAINS :],
    )
    width = halves_ref.shape[1]
    depth = low_ref.shape[1] // TILE
    step = pl.program_id(0)

    @pl.when(step == 0)
    def _():
        shards, _, wide = tiles_ref.shape[1:]
        copies = []
        for i in range(ranks):
            shard = pl.ds(source_ref[r * ranks + i] * shards, shards)
            copies.append(pltpu.make_async_copy(amp_ref.at[shard], tiles_ref.at[i], ready.at[i]))
            copies[i].start()
        for k in range(depth):
            count_ref[k] = 0
        for i in range(ranks):
            copies[i].wait()
            for shard in range(shards):
                for tile in range(wide // TILE):
                    k = shard * (wide // TILE) + tile

                    @pl.when(row_flag_ref[tile_ref[r * ranks + i], k] != 0)
                    def _():
                        count = count_ref[k]
                        row_ref[k * ranks + count] = i
                        count_ref[k] = count + 1
                        rows = pl.ds(pl.multiple_of(count * TILE_ROWS, TILE_ROWS), TILE_ROWS)
                        value = tiles_ref[i, shard, :, pl.ds(tile * TILE, TILE)]
                        high = value.astype(jnp.bfloat16)
                        twice_ref[rows, pl.ds(2 * k * TILE, TILE)] = high
                        twice_ref[rows, pl.ds((2 * k + 1) * TILE, TILE)] = high
                        low_ref[rows, pl.ds(k * TILE, TILE)] = (value - high.astype(jnp.float32)).astype(
                            jnp.bfloat16
                        )

    total_ref[...] = jnp.zeros_like(total_ref)
    for k in range(depth):
        needed = flag_ref[k, (first + step) * width // TILE] != 0
        for count in range(1, ranks + 1):

            @pl.when(jnp.logical_and(needed, count_ref[k] == count))
            def _():
                rows = pl.ds(0, count * TILE_ROWS)
                deep = pl.ds(2 * k * TILE, 2 * TILE)
                part = jnp.dot(
                    low_ref[rows, pl.ds(k * TILE, TILE)],
                    halves_ref[pl.ds(2 * k * TILE, TILE), :],
                    preferred_element_type=jnp.float32,
                )
                part = part + jnp.dot(
                    twice_ref[rows, deep], halves_ref[deep, :], preferred_element_type=jnp.float32
                )
                for j in range(count):
                    at = pl.ds(pl.multiple_of(row_ref[k * ranks + j] * TILE_ROWS, TILE_ROWS), TILE_ROWS)
                    total_ref[at, :] += part[j * TILE_ROWS : (j + 1) * TILE_ROWS]

    share = width // CHAINS
    for chain, (kept, sent) in enumerate(RANKS):
        columns = pl.ds(chain * share, share)
        for ref, peers in ((out_refs[2 * chain], kept), (out_refs[2 * chain + 1], sent)):
            for i, peer in enumerate(peers):
                ref[i] = total_ref[pl.ds(peer * TILE_ROWS, TILE_ROWS), columns]


def product(r, first, steps, ranks, source, tile, row_flags, int_tiles, gathered, halves):
    depth, width = halves.shape[0] // 2, halves.shape[1]
    shards = depth // gathered.shape[2]
    rows = ranks * TILE_ROWS
    share = COLUMNS // CHAINS

    integral = pl.BlockSpec((2 * depth, COLUMNS), lambda i, *_: (0, first + i))
    return pl.pallas_call(
        functools.partial(product_kernel, r, first, ranks),
        out_shape=[jax.ShapeDtypeStruct((2, TILE_ROWS, share * steps), jnp.float32)] * (2 * CHAINS),
        grid_spec=pltpu.PrefetchScalarGridSpec(
            num_scalar_prefetch=4,
            grid=(steps,),
            in_specs=[pl.BlockSpec(memory_space=pl.ANY), integral],
            out_specs=[pl.BlockSpec((2, TILE_ROWS, share), lambda i, *_: (0, 0, i))] * (2 * CHAINS),
            scratch_shapes=[
                pltpu.VMEM((ranks, shards, TILE_ROWS, depth // shards), jnp.float32),
                pltpu.VMEM((rows, 2 * depth), jnp.bfloat16),
                pltpu.VMEM((rows, depth), jnp.bfloat16),
                pltpu.VMEM((rows, COLUMNS), jnp.float32),
                pltpu.SMEM((depth // TILE,), jnp.int32),
                pltpu.SMEM((depth // TILE * ranks,), jnp.int32),
                pltpu.SemaphoreType.DMA((ranks,)),
            ],
        ),
        compiler_params=pltpu.CompilerParams(vmem_limit_bytes=VMEM_BYTES),
        cost_estimate=pl.CostEstimate(
            flops=6 * rows * depth * steps * COLUMNS, bytes_accessed=4 * depth * steps * COLUMNS, transcendentals=0
        ),
    )(source, tile, row_flags, int_tiles, gathered, halves)


def relay_kernel(*refs):
    for chain in range(CHAINS):
        refs[2 * CHAINS + chain][...] = refs[2 * chain][0] + refs[2 * chain + 1][0]


def relay(kept, heard):
    _, rows, width = kept[0].shape
    passed = pl.BlockSpec((1, rows, width), lambda i: (1, 0, 0))
    out = jax.ShapeDtypeStruct((rows, width), jnp.float32)
    return pl.pallas_call(
        relay_kernel,
        out_shape=[out] * CHAINS,
        grid=(1,),
        in_specs=[passed] * (2 * CHAINS),
        out_specs=[pl.BlockSpec((rows, width), lambda i: (0, 0))] * CHAINS,
    )(*[array for pair in zip(kept, heard) for array in pair])


def finish_kernel(columns, *refs):
    refs = refs[1:]
    parts, (term_ref, denominator_ref), out_ref = refs[: 3 * CHAINS], refs[3 * CHAINS : 3 * CHAINS + 2], refs[-1]
    share = columns // CHAINS
    for block in range(term_ref.shape[1] // columns):
        for chain in range(CHAINS):
            kept, heard, relayed = parts[3 * chain : 3 * chain + 3]
            source = pl.ds(block * share, share)
            target = pl.ds(block * columns + chain * share, share)
            total = kept[0, :, source] + heard[0, :, source] + relayed[:, source]
            out_ref[:, target] = (total + term_ref[:, target]) / denominator_ref[:, target]


def finish(r, start, slot, kept, heard, relayed, other_terms, denominators, update):
    blocks = 2 if start == 0 else 1
    share = kept[0].shape[2] // blocks
    width = share * CHAINS
    first = pl.BlockSpec((1, TILE_ROWS, share), lambda i, slot: (0, 0, i))
    whole = pl.BlockSpec((TILE_ROWS, share), lambda i, slot: (0, i))
    owned = pl.BlockSpec((TILE_ROWS, width), lambda i, slot: (slot[r], start * COLUMNS // width + i))
    before = [] if update is None else [update]
    return pl.pallas_call(
        functools.partial(finish_kernel, COLUMNS),
        out_shape=jax.ShapeDtypeStruct(other_terms.shape, jnp.float32),
        grid_spec=pltpu.PrefetchScalarGridSpec(
            num_scalar_prefetch=1,
            grid=(blocks,),
            in_specs=[first, first, whole] * CHAINS
            + [owned, owned]
            + [pl.BlockSpec(memory_space=pl.ANY)] * len(before),
            out_specs=owned,
        ),
        input_output_aliases={3 * CHAINS + 3: 0} if before else {},
        cost_estimate=pl.CostEstimate(flops=0, bytes_accessed=24 * TILE_ROWS * width, transcendentals=0),
    )(
        slot,
        *[array for chain in zip(kept, heard, relayed) for array in chain],
        other_terms,
        denominators,
        *before,
    )


def in_rounds(devices, ranks, amplitudes, amp_tiles, integrals, int_tiles, owner_tiles, other_terms, denominators):
    rank = lax.axis_index("cd").astype(jnp.int32)
    spot = lax.axis_index("ab").astype(jnp.int32)
    tiles = amp_tiles.shape[1]
    half = tiles // CORES

    def gather(array):
        return lax.all_gather(array, "ab", axis=0)

    def swap(sent, peers):
        return [lax.ppermute(array, "cd", [(c, c ^ peer) for c in range(ranks)]) for array, peer in zip(sent, peers)]

    where, source, slot, tile = plan(owner_tiles, jnp.stack([rank, spot]), devices, half)
    whole = take(FIRST, tiles, where, amp_tiles, amplitudes)
    halves = split(integrals)
    away = take(AWAY, half, where, amp_tiles, amplitudes)
    stay = take(STAY, half, where, amp_tiles, amplitudes)
    came = lax.ppermute(away, "ab", [(i, i ^ 1) for i in range(devices)])
    mine = where[WHOSE] == 0
    shards = [whole, jnp.where(mine, stay, came), jnp.where(mine, came, stay)]
    gathered = [gather(shard) for shard in shards]
    terms = (other_terms, denominators)
    tie = lax.optimization_barrier
    steps = halves.shape[1] // COLUMNS
    most = steps * 3 // 4

    def begin(r, rows, first=0, count=steps):
        return product(r, first, count, ranks, source, tile, row_flags, int_tiles, rows, halves)

    def send(parts):
        return swap(parts[1::2], (1, 2))

    def pass_on(parts, heard):
        onward = relay(parts[0::2], heard)
        return onward, swap(onward, (2, 1))

    row_flags, halves = tie((amp_tiles, halves))
    for bit in range((devices - 1).bit_length()):
        reach = 1 << bit
        came = lax.ppermute(row_flags, "ab", [(i, i ^ reach) for i in range(devices)])
        row_flags = jnp.where(
            spot & reach == 0, jnp.concatenate([row_flags, came]), jnp.concatenate([came, row_flags])
        )
    rows, halves, row_flags, *_ = tie((gathered[0], halves, row_flags, *shards[1:]))
    parts0 = begin(0, rows)
    heard0 = send(parts0)
    parts1, heard0 = tie((begin(1, rows), heard0))
    heard1 = send(parts1)
    onward, relayed0 = pass_on(parts0, heard0)

    onward, relayed1 = pass_on(parts1, heard1)
    rows, onward = tie((gathered[1], onward))
    parts2, relayed0, relayed1 = tie((begin(2, rows), relayed0, relayed1))
    parts2, slot, onward = tie((parts2, slot, onward))
    heard2 = send(parts2)
    update = finish(0, 0, slot, parts0[0::2], heard0, relayed0, *terms, None)
    update = finish(1, 0, slot, parts1[0::2], heard1, relayed1, *terms, update)
    heard2, update = tie((heard2, update))
    onward, relayed2 = pass_on(parts2, heard2)

    rows, onward, update = tie((gathered[2], onward, update))
    parts3, relayed2 = tie((begin(3, rows, 0, most), relayed2))
    heard3 = send(parts3)
    parts4, heard3 = tie((begin(3, rows, most, steps - most), heard3))
    heard4 = send(parts4)
    onward, relayed3 = pass_on(parts3, heard3)
    slot, onward = tie((slot, onward))
    update = finish(2, 0, slot, parts2[0::2], heard2, relayed2, *terms, update)
    heard4, update = tie((heard4, update))
    _, relayed4 = pass_on(parts4, heard4)
    update = finish(3, 0, slot, parts3[0::2], heard3, relayed3, *terms, update)
    return finish(3, most, slot, parts4[0::2], heard4, relayed4, *terms, update)


def solution(mesh):
    ranks, places = mesh.shape["cd"], mesh.shape["ab"]

    def on_device(amplitudes, amp_tiles, integrals, int_tiles, owner_tiles, other_terms, denominators):
        args = (amplitudes, amp_tiles, integrals, int_tiles, owner_tiles, other_terms, denominators)
        tiles = owner_tiles.shape[0]
        whole = places % CORES == 0 and amplitudes.shape[1] % (CORES * TILE) == 0
        if whole and ranks == 4 and tiles == 2 * places == ROUNDS * ranks:
            return in_rounds(places, ranks, *args)
        return plain(*args)

    return jax.shard_map(
        on_device,
        mesh=mesh,
        in_specs=(
            P("ab", "cd"),
            P("ab", "cd"),
            P("cd", "ab"),
            P("cd", "ab"),
            P(),
            P("cd", "ab"),
            P("cd", "ab"),
        ),
        out_specs=P("cd", "ab"),
        check_vma=False,
    )
```

```python
import functools

import jax
import jax.numpy as jnp
from jax import lax
from jax.experimental import pallas as pl
from jax.experimental.pallas import tpu as pltpu
from jax.sharding import PartitionSpec as P

TILE = 1024
TILE_ROWS = 128
CORES = 2
VMEM_BYTES = 58 * 1024 * 1024
COLUMNS = 256
ROUNDS = 4
FIRST, AWAY, STAY, WHOSE = 0, 2, 4, 6
CHAINS = 2
RANKS = (((0, 2), (1, 3)), ((0, 1), (2, 3)))


def spread_tiles(tile_flags, row_span, col_span):
    tile_rows, tile_cols = tile_flags.shape
    values = tile_flags.astype(jnp.float32)
    return jnp.broadcast_to(
        values[:, None, :, None], (tile_rows, row_span, tile_cols, col_span)
    ).reshape(tile_rows * row_span, tile_cols * col_span)


def plain(amplitudes, amp_tiles, integrals, int_tiles, owner_tiles, other_terms, denominators):
    masked_ints = integrals * spread_tiles(int_tiles, TILE, TILE)
    masked_amps = amplitudes * spread_tiles(amp_tiles, TILE_ROWS, TILE)
    tile_count = owner_tiles.shape[0]
    gathered = lax.all_gather(masked_amps, "ab", axis=0, tiled=True)
    partial_value = jnp.dot(
        gathered, masked_ints, precision=lax.Precision.HIGHEST, preferred_element_type=jnp.float32
    )
    col_width = partial_value.shape[1]
    partial_value = partial_value.reshape(tile_count, TILE_ROWS, col_width)[owner_tiles].reshape(
        tile_count * TILE_ROWS, col_width
    )
    owned = lax.psum_scatter(partial_value, "cd", scatter_dimension=0, tiled=True)
    return (owned + other_terms) / denominators


def plan_kernel(devices, half, owner_ref, here_ref, take_ref, source_ref, slot_ref, tile_ref, *scratch):
    inverse_ref, color_ref, pair_ref, device_ref, late_ref = scratch
    rank, spot = here_ref[0], here_ref[1]
    ranks = devices * 2 // ROUNDS
    for q in range(2 * devices):
        inverse_ref[owner_ref[q]] = q
        color_ref[q] = -1
    for d in range(devices):
        late_ref[d] = -1

    def walk(first, colors_ref, after):
        def step(state):
            at, _ = state
            colors_ref[at] = 0
            colors_ref[at ^ 1] = 1
            following = after(at ^ 1)
            return following, colors_ref[following]

        lax.while_loop(lambda state: state[1] < 0, step, (jnp.int32(first), colors_ref[first]))

    for t in range(0, 2 * devices, 2):
        walk(t, color_ref, lambda u: owner_ref[inverse_ref[u] ^ 1])
    for c in range(ranks):
        for p in range(2):
            q = ROUNDS * c + 2 * p
            second = color_ref[owner_ref[q]]
            source_ref[p * ranks + (c ^ rank)] = owner_ref[q + second] >> 1
            tile_ref[p * ranks + (c ^ rank)] = owner_ref[q + second]
            group = 2 * c + p
            device = owner_ref[q + 1 - second] >> 1
            device_ref[group] = device
            pair_ref[device] = group

            @pl.when(rank == c)
            def _():
                slot_ref[p] = 2 * p + second
                slot_ref[2 + p] = 2 * p + 1 - second

    for d in range(0, devices, 2):
        walk(d, late_ref, lambda u: device_ref[pair_ref[u] ^ 1])
    for c in range(ranks):
        swap = late_ref[device_ref[2 * c]]
        for p in range(2):
            r = 2 + (swap ^ p)
            device = device_ref[2 * c + p]
            source_ref[r * ranks + (c ^ rank)] = device >> 1
            tile_ref[r * ranks + (c ^ rank)] = 2 * device + 1 - color_ref[2 * device]

        @pl.when(jnp.logical_and(rank == c, swap != 0))
        def _():
            kept = slot_ref[2]
            slot_ref[2] = slot_ref[3]
            slot_ref[3] = kept

    early = color_ref[2 * spot]
    core = spot % CORES
    take_ref[FIRST] = early
    take_ref[FIRST + 1] = 0
    take_ref[AWAY] = 1 - early
    take_ref[AWAY + 1] = (1 - core) * half
    take_ref[STAY] = 1 - early
    take_ref[STAY + 1] = core * half
    take_ref[WHOSE] = late_ref[spot]


def plan(owner_tiles, here, devices, half):
    tiles = 2 * devices
    smem = pl.BlockSpec(memory_space=pltpu.SMEM)
    ints = jnp.int32
    return pl.pallas_call(
        functools.partial(plan_kernel, devices, half),
        out_shape=(
            jax.ShapeDtypeStruct((WHOSE + 1,), ints),
            jax.ShapeDtypeStruct((tiles,), ints),
            jax.ShapeDtypeStruct((ROUNDS,), ints),
            jax.ShapeDtypeStruct((tiles,), ints),
        ),
        in_specs=[smem, smem],
        out_specs=(smem, smem, smem, smem),
        scratch_shapes=[pltpu.SMEM((tiles,), ints)] * 2 + [pltpu.SMEM((devices,), ints)] * 3,
    )(owner_tiles, here)


def take_kernel(at, take_ref, flag_ref, amp_ref, out_ref):
    flag = flag_ref[take_ref[at], take_ref[at + 1] + pl.program_id(0)]
    out_ref[...] = amp_ref[...] * flag.astype(jnp.float32)


def take(at, tiles, where, amp_tiles, amplitudes):
    return pl.pallas_call(
        functools.partial(take_kernel, at),
        out_shape=jax.ShapeDtypeStruct((TILE_ROWS, tiles * TILE), jnp.float32),
        grid_spec=pltpu.PrefetchScalarGridSpec(
            num_scalar_prefetch=2,
            grid=(tiles,),
            in_specs=[
                pl.BlockSpec((TILE_ROWS, TILE), lambda j, where, flags: (where[at], where[at + 1] + j))
            ],
            out_specs=pl.BlockSpec((TILE_ROWS, TILE), lambda j, where, flags: (0, j)),
        ),
    )(where, amp_tiles, amplitudes)


def split_kernel(value_ref, halves_ref):
    value = value_ref[...]
    high = value.astype(jnp.bfloat16)
    halves_ref[:TILE, :] = high
    halves_ref[TILE:, :] = (value - high.astype(jnp.float32)).astype(jnp.bfloat16)


def split(integrals):
    depth, width = integrals.shape
    return pl.pallas_call(
        split_kernel,
        out_shape=jax.ShapeDtypeStruct((2 * depth, width), jnp.bfloat16),
        grid=(depth // TILE, width // TILE),
        in_specs=[pl.BlockSpec((TILE, TILE), lambda i, j: (i, j))],
        out_specs=pl.BlockSpec((2 * TILE, TILE), lambda i, j: (i, j)),
        compiler_params=pltpu.CompilerParams(vmem_limit_bytes=VMEM_BYTES),
        cost_estimate=pl.CostEstimate(flops=0, bytes_accessed=8 * depth * width, transcendentals=0),
    )(integrals)


def product_kernel(r, first, ranks, source_ref, tile_ref, row_flag_ref, flag_ref, amp_ref, halves_ref, *refs):
    out_refs, (tiles_ref, twice_ref, low_ref, total_ref, count_ref, row_ref, ready) = (
        refs[: 2 * CHAINS],
        refs[2 * CHAINS :],
    )
    width = halves_ref.shape[1]
    depth = low_ref.shape[1] // TILE
    step = pl.program_id(0)

    @pl.when(step == 0)
    def _():
        shards, _, wide = tiles_ref.shape[1:]
        copies = []
        for i in range(ranks):
            shard = pl.ds(source_ref[r * ranks + i] * shards, shards)
            copies.append(pltpu.make_async_copy(amp_ref.at[shard], tiles_ref.at[i], ready.at[i]))
            copies[i].start()
        for k in range(depth):
            count_ref[k] = 0
        for i in range(ranks):
            copies[i].wait()
            for shard in range(shards):
                for tile in range(wide // TILE):
                    k = shard * (wide // TILE) + tile

                    @pl.when(row_flag_ref[tile_ref[r * ranks + i], k] != 0)
                    def _():
                        count = count_ref[k]
                        row_ref[k * ranks + count] = i
                        count_ref[k] = count + 1
                        rows = pl.ds(pl.multiple_of(count * TILE_ROWS, TILE_ROWS), TILE_ROWS)
                        value = tiles_ref[i, shard, :, pl.ds(tile * TILE, TILE)]
                        high = value.astype(jnp.bfloat16)
                        twice_ref[rows, pl.ds(2 * k * TILE, TILE)] = high
                        twice_ref[rows, pl.ds((2 * k + 1) * TILE, TILE)] = high
                        low_ref[rows, pl.ds(k * TILE, TILE)] = (value - high.astype(jnp.float32)).astype(
                            jnp.bfloat16
                        )

    total_ref[...] = jnp.zeros_like(total_ref)

    @pl.loop(0, depth)
    def _(k):
        needed = flag_ref[k, (first + step) * width // TILE] != 0
        here = pl.ds(pl.multiple_of(k * TILE, TILE), TILE)
        top = pl.ds(pl.multiple_of(2 * k * TILE, TILE), TILE)
        deep = pl.ds(pl.multiple_of(2 * k * TILE, TILE), 2 * TILE)
        for count in range(1, ranks + 1):

            @pl.when(jnp.logical_and(needed, count_ref[k] == count))
            def _():
                rows = pl.ds(0, count * TILE_ROWS)
                part = jnp.dot(low_ref[rows, here], halves_ref[top, :], preferred_element_type=jnp.float32)
                part = part + jnp.dot(
                    twice_ref[rows, deep], halves_ref[deep, :], preferred_element_type=jnp.float32
                )
                for j in range(count):
                    at = pl.ds(pl.multiple_of(row_ref[k * ranks + j] * TILE_ROWS, TILE_ROWS), TILE_ROWS)
                    total_ref[at, :] += part[j * TILE_ROWS : (j + 1) * TILE_ROWS]

    share = width // CHAINS
    for chain, (kept, sent) in enumerate(RANKS):
        columns = pl.ds(chain * share, share)
        for ref, peers in ((out_refs[2 * chain], kept), (out_refs[2 * chain + 1], sent)):
            for i, peer in enumerate(peers):
                ref[i] = total_ref[pl.ds(peer * TILE_ROWS, TILE_ROWS), columns]


def product(r, first, steps, ranks, source, tile, row_flags, int_tiles, gathered, halves):
    depth, width = halves.shape[0] // 2, halves.shape[1]
    shards = depth // gathered.shape[2]
    rows = ranks * TILE_ROWS
    share = COLUMNS // CHAINS

    integral = pl.BlockSpec((2 * depth, COLUMNS), lambda i, *_: (0, first + i))
    return pl.pallas_call(
        functools.partial(product_kernel, r, first, ranks),
        out_shape=[jax.ShapeDtypeStruct((2, TILE_ROWS, share * steps), jnp.float32)] * (2 * CHAINS),
        grid_spec=pltpu.PrefetchScalarGridSpec(
            num_scalar_prefetch=4,
            grid=(steps,),
            in_specs=[pl.BlockSpec(memory_space=pl.ANY), integral],
            out_specs=[pl.BlockSpec((2, TILE_ROWS, share), lambda i, *_: (0, 0, i))] * (2 * CHAINS),
            scratch_shapes=[
                pltpu.VMEM((ranks, shards, TILE_ROWS, depth // shards), jnp.float32),
                pltpu.VMEM((rows, 2 * depth), jnp.bfloat16),
                pltpu.VMEM((rows, depth), jnp.bfloat16),
                pltpu.VMEM((rows, COLUMNS), jnp.float32),
                pltpu.SMEM((depth // TILE,), jnp.int32),
                pltpu.SMEM((depth // TILE * ranks,), jnp.int32),
                pltpu.SemaphoreType.DMA((ranks,)),
            ],
        ),
        compiler_params=pltpu.CompilerParams(vmem_limit_bytes=VMEM_BYTES),
        cost_estimate=pl.CostEstimate(
            flops=6 * rows * depth * steps * COLUMNS, bytes_accessed=4 * depth * steps * COLUMNS, transcendentals=0
        ),
    )(source, tile, row_flags, int_tiles, gathered, halves)


def relay_kernel(*refs):
    for chain in range(CHAINS):
        refs[2 * CHAINS + chain][...] = refs[2 * chain][0] + refs[2 * chain + 1][0]


def relay(kept, heard):
    _, rows, width = kept[0].shape
    passed = pl.BlockSpec((1, rows, width), lambda i: (1, 0, 0))
    out = jax.ShapeDtypeStruct((rows, width), jnp.float32)
    return pl.pallas_call(
        relay_kernel,
        out_shape=[out] * CHAINS,
        grid=(1,),
        in_specs=[passed] * (2 * CHAINS),
        out_specs=[pl.BlockSpec((rows, width), lambda i: (0, 0))] * CHAINS,
    )(*[array for pair in zip(kept, heard) for array in pair])


def finish_kernel(columns, *refs):
    refs = refs[1:]
    parts, (term_ref, denominator_ref), out_ref = refs[: 3 * CHAINS], refs[3 * CHAINS : 3 * CHAINS + 2], refs[-1]
    share = columns // CHAINS
    for block in range(term_ref.shape[1] // columns):
        for chain in range(CHAINS):
            kept, heard, relayed = parts[3 * chain : 3 * chain + 3]
            source = pl.ds(block * share, share)
            target = pl.ds(block * columns + chain * share, share)
            total = kept[0, :, source] + heard[0, :, source] + relayed[:, source]
            out_ref[:, target] = (total + term_ref[:, target]) / denominator_ref[:, target]


def finish(r, start, slot, kept, heard, relayed, other_terms, denominators, update):
    blocks = 2 if start == 0 else 1
    share = kept[0].shape[2] // blocks
    width = share * CHAINS
    first = pl.BlockSpec((1, TILE_ROWS, share), lambda i, slot: (0, 0, i))
    whole = pl.BlockSpec((TILE_ROWS, share), lambda i, slot: (0, i))
    owned = pl.BlockSpec((TILE_ROWS, width), lambda i, slot: (slot[r], start * COLUMNS // width + i))
    before = [] if update is None else [update]
    return pl.pallas_call(
        functools.partial(finish_kernel, COLUMNS),
        out_shape=jax.ShapeDtypeStruct(other_terms.shape, jnp.float32),
        grid_spec=pltpu.PrefetchScalarGridSpec(
            num_scalar_prefetch=1,
            grid=(blocks,),
            in_specs=[first, first, whole] * CHAINS
            + [owned, owned]
            + [pl.BlockSpec(memory_space=pl.ANY)] * len(before),
            out_specs=owned,
        ),
        input_output_aliases={3 * CHAINS + 3: 0} if before else {},
        cost_estimate=pl.CostEstimate(flops=0, bytes_accessed=24 * TILE_ROWS * width, transcendentals=0),
    )(
        slot,
        *[array for chain in zip(kept, heard, relayed) for array in chain],
        other_terms,
        denominators,
        *before,
    )


def in_rounds(devices, ranks, amplitudes, amp_tiles, integrals, int_tiles, owner_tiles, other_terms, denominators):
    rank = lax.axis_index("cd").astype(jnp.int32)
    spot = lax.axis_index("ab").astype(jnp.int32)
    tiles = amp_tiles.shape[1]
    half = tiles // CORES

    def gather(array):
        return lax.all_gather(array, "ab", axis=0)

    def swap(sent, peers):
        return [lax.ppermute(array, "cd", [(c, c ^ peer) for c in range(ranks)]) for array, peer in zip(sent, peers)]

    where, source, slot, tile = plan(owner_tiles, jnp.stack([rank, spot]), devices, half)
    whole = take(FIRST, tiles, where, amp_tiles, amplitudes)
    halves = split(integrals)
    away = take(AWAY, half, where, amp_tiles, amplitudes)
    stay = take(STAY, half, where, amp_tiles, amplitudes)
    came = lax.ppermute(away, "ab", [(i, i ^ 1) for i in range(devices)])
    mine = where[WHOSE] == 0
    shards = [whole, jnp.where(mine, stay, came), jnp.where(mine, came, stay)]
    gathered = [gather(shard) for shard in shards]
    terms = (other_terms, denominators)
    tie = lax.optimization_barrier
    steps = halves.shape[1] // COLUMNS
    most = steps * 3 // 4

    def begin(r, rows, first=0, count=steps):
        return product(r, first, count, ranks, source, tile, row_flags, int_tiles, rows, halves)

    def send(parts):
        return swap(parts[1::2], (1, 2))

    def pass_on(parts, heard):
        onward = relay(parts[0::2], heard)
        return onward, swap(onward, (2, 1))

    row_flags, halves = tie((amp_tiles, halves))
    for bit in range((devices - 1).bit_length()):
        reach = 1 << bit
        came = lax.ppermute(row_flags, "ab", [(i, i ^ reach) for i in range(devices)])
        row_flags = jnp.where(
            spot & reach == 0, jnp.concatenate([row_flags, came]), jnp.concatenate([came, row_flags])
        )
    rows, halves, row_flags, *_ = tie((gathered[0], halves, row_flags, *shards[1:]))
    parts0 = begin(0, rows)
    heard0 = send(parts0)
    parts1, heard0 = tie((begin(1, rows), heard0))
    heard1 = send(parts1)
    onward, relayed0 = pass_on(parts0, heard0)

    onward, relayed1 = pass_on(parts1, heard1)
    rows, onward = tie((gathered[1], onward))
    parts2, relayed0, relayed1 = tie((begin(2, rows), relayed0, relayed1))
    parts2, slot, onward = tie((parts2, slot, onward))
    heard2 = send(parts2)
    update = finish(0, 0, slot, parts0[0::2], heard0, relayed0, *terms, None)
    update = finish(1, 0, slot, parts1[0::2], heard1, relayed1, *terms, update)
    heard2, update = tie((heard2, update))
    onward, relayed2 = pass_on(parts2, heard2)

    rows, onward, update = tie((gathered[2], onward, update))
    parts3, relayed2 = tie((begin(3, rows, 0, most), relayed2))
    heard3 = send(parts3)
    parts4, heard3 = tie((begin(3, rows, most, steps - most), heard3))
    heard4 = send(parts4)
    onward, relayed3 = pass_on(parts3, heard3)
    slot, onward = tie((slot, onward))
    update = finish(2, 0, slot, parts2[0::2], heard2, relayed2, *terms, update)
    heard4, update = tie((heard4, update))
    _, relayed4 = pass_on(parts4, heard4)
    update = finish(3, 0, slot, parts3[0::2], heard3, relayed3, *terms, update)
    return finish(3, most, slot, parts4[0::2], heard4, relayed4, *terms, update)


def solution(mesh):
    ranks, places = mesh.shape["cd"], mesh.shape["ab"]

    def on_device(amplitudes, amp_tiles, integrals, int_tiles, owner_tiles, other_terms, denominators):
        args = (amplitudes, amp_tiles, integrals, int_tiles, owner_tiles, other_terms, denominators)
        tiles = owner_tiles.shape[0]
        whole = places % CORES == 0 and amplitudes.shape[1] % (CORES * TILE) == 0
        if whole and ranks == 4 and tiles == 2 * places == ROUNDS * ranks:
            return in_rounds(places, ranks, *args)
        return plain(*args)

    return jax.shard_map(
        on_device,
        mesh=mesh,
        in_specs=(
            P("ab", "cd"),
            P("ab", "cd"),
            P("cd", "ab"),
            P("cd", "ab"),
            P(),
            P("cd", "ab"),
            P("cd", "ab"),
        ),
        out_specs=P("cd", "ab"),
        check_vma=False,
    )
```

```python
import functools

import jax
import jax.numpy as jnp
from jax import lax
from jax.experimental import pallas as pl
from jax.experimental.pallas import tpu as pltpu
from jax.sharding import PartitionSpec as P

TILE = 1024
TILE_ROWS = 128
CORES = 2
VMEM_BYTES = 58 * 1024 * 1024
COLUMNS = 256
ROUNDS = 4
FIRST, AWAY, STAY, WHOSE = 0, 2, 4, 6
CHAINS = 2
RANKS = (((0, 2), (1, 3)), ((0, 1), (2, 3)))


def spread_tiles(tile_flags, row_span, col_span):
    tile_rows, tile_cols = tile_flags.shape
    values = tile_flags.astype(jnp.float32)
    return jnp.broadcast_to(
        values[:, None, :, None], (tile_rows, row_span, tile_cols, col_span)
    ).reshape(tile_rows * row_span, tile_cols * col_span)


def plain(amplitudes, amp_tiles, integrals, int_tiles, owner_tiles, other_terms, denominators):
    masked_ints = integrals * spread_tiles(int_tiles, TILE, TILE)
    masked_amps = amplitudes * spread_tiles(amp_tiles, TILE_ROWS, TILE)
    tile_count = owner_tiles.shape[0]
    gathered = lax.all_gather(masked_amps, "ab", axis=0, tiled=True)
    partial_value = jnp.dot(
        gathered, masked_ints, precision=lax.Precision.HIGHEST, preferred_element_type=jnp.float32
    )
    col_width = partial_value.shape[1]
    partial_value = partial_value.reshape(tile_count, TILE_ROWS, col_width)[owner_tiles].reshape(
        tile_count * TILE_ROWS, col_width
    )
    owned = lax.psum_scatter(partial_value, "cd", scatter_dimension=0, tiled=True)
    return (owned + other_terms) / denominators


def plan_kernel(devices, half, owner_ref, here_ref, take_ref, source_ref, slot_ref, tile_ref, *scratch):
    inverse_ref, color_ref, pair_ref, device_ref, late_ref = scratch
    rank, spot = here_ref[0], here_ref[1]
    ranks = devices * 2 // ROUNDS
    for q in range(2 * devices):
        inverse_ref[owner_ref[q]] = q
        color_ref[q] = -1
    for d in range(devices):
        late_ref[d] = -1

    def walk(first, colors_ref, after):
        def step(state):
            at, _ = state
            colors_ref[at] = 0
            colors_ref[at ^ 1] = 1
            following = after(at ^ 1)
            return following, colors_ref[following]

        lax.while_loop(lambda state: state[1] < 0, step, (jnp.int32(first), colors_ref[first]))

    for t in range(0, 2 * devices, 2):
        walk(t, color_ref, lambda u: owner_ref[inverse_ref[u] ^ 1])
    for c in range(ranks):
        for p in range(2):
            q = ROUNDS * c + 2 * p
            second = color_ref[owner_ref[q]]
            source_ref[p * ranks + (c ^ rank)] = owner_ref[q + second] >> 1
            tile_ref[p * ranks + (c ^ rank)] = owner_ref[q + second]
            group = 2 * c + p
            device = owner_ref[q + 1 - second] >> 1
            device_ref[group] = device
            pair_ref[device] = group

            @pl.when(rank == c)
            def _():
                slot_ref[p] = 2 * p + second
                slot_ref[2 + p] = 2 * p + 1 - second

    for d in range(0, devices, 2):
        walk(d, late_ref, lambda u: device_ref[pair_ref[u] ^ 1])
    for c in range(ranks):
        swap = late_ref[device_ref[2 * c]]
        for p in range(2):
            r = 2 + (swap ^ p)
            device = device_ref[2 * c + p]
            source_ref[r * ranks + (c ^ rank)] = device >> 1
            tile_ref[r * ranks + (c ^ rank)] = 2 * device + 1 - color_ref[2 * device]

        @pl.when(jnp.logical_and(rank == c, swap != 0))
        def _():
            kept = slot_ref[2]
            slot_ref[2] = slot_ref[3]
            slot_ref[3] = kept

    early = color_ref[2 * spot]
    core = spot % CORES
    take_ref[FIRST] = early
    take_ref[FIRST + 1] = 0
    take_ref[AWAY] = 1 - early
    take_ref[AWAY + 1] = (1 - core) * half
    take_ref[STAY] = 1 - early
    take_ref[STAY + 1] = core * half
    take_ref[WHOSE] = late_ref[spot]


def plan(owner_tiles, here, devices, half):
    tiles = 2 * devices
    smem = pl.BlockSpec(memory_space=pltpu.SMEM)
    ints = jnp.int32
    return pl.pallas_call(
        functools.partial(plan_kernel, devices, half),
        out_shape=(
            jax.ShapeDtypeStruct((WHOSE + 1,), ints),
            jax.ShapeDtypeStruct((tiles,), ints),
            jax.ShapeDtypeStruct((ROUNDS,), ints),
            jax.ShapeDtypeStruct((tiles,), ints),
        ),
        in_specs=[smem, smem],
        out_specs=(smem, smem, smem, smem),
        scratch_shapes=[pltpu.SMEM((tiles,), ints)] * 2 + [pltpu.SMEM((devices,), ints)] * 3,
    )(owner_tiles, here)


def take_kernel(at, take_ref, flag_ref, amp_ref, out_ref):
    flag = flag_ref[take_ref[at], take_ref[at + 1] + pl.program_id(0)]
    out_ref[...] = amp_ref[...] * flag.astype(jnp.float32)


def take(at, tiles, where, amp_tiles, amplitudes):
    return pl.pallas_call(
        functools.partial(take_kernel, at),
        out_shape=jax.ShapeDtypeStruct((TILE_ROWS, tiles * TILE), jnp.float32),
        grid_spec=pltpu.PrefetchScalarGridSpec(
            num_scalar_prefetch=2,
            grid=(tiles,),
            in_specs=[
                pl.BlockSpec((TILE_ROWS, TILE), lambda j, where, flags: (where[at], where[at + 1] + j))
            ],
            out_specs=pl.BlockSpec((TILE_ROWS, TILE), lambda j, where, flags: (0, j)),
        ),
    )(where, amp_tiles, amplitudes)


def split_kernel(value_ref, halves_ref):
    value = value_ref[...]
    high = value.astype(jnp.bfloat16)
    halves_ref[:TILE, :] = high
    halves_ref[TILE:, :] = (value - high.astype(jnp.float32)).astype(jnp.bfloat16)


def split(integrals):
    depth, width = integrals.shape
    return pl.pallas_call(
        split_kernel,
        out_shape=jax.ShapeDtypeStruct((2 * depth, width), jnp.bfloat16),
        grid=(depth // TILE, width // TILE),
        in_specs=[pl.BlockSpec((TILE, TILE), lambda i, j: (i, j))],
        out_specs=pl.BlockSpec((2 * TILE, TILE), lambda i, j: (i, j)),
        compiler_params=pltpu.CompilerParams(vmem_limit_bytes=VMEM_BYTES),
        cost_estimate=pl.CostEstimate(flops=0, bytes_accessed=8 * depth * width, transcendentals=0),
    )(integrals)


def product_kernel(r, first, ranks, source_ref, tile_ref, row_flag_ref, flag_ref, amp_ref, halves_ref, *refs):
    out_refs, (tiles_ref, twice_ref, low_ref, total_ref, count_ref, row_ref, ready) = (
        refs[: 2 * CHAINS],
        refs[2 * CHAINS :],
    )
    width = halves_ref.shape[1]
    depth = low_ref.shape[1] // TILE
    step = pl.program_id(0)

    @pl.when(step == 0)
    def _():
        shards, _, wide = tiles_ref.shape[1:]
        copies = []
        for i in range(ranks):
            shard = pl.ds(source_ref[r * ranks + i] * shards, shards)
            copies.append(pltpu.make_async_copy(amp_ref.at[shard], tiles_ref.at[i], ready.at[i]))
            copies[i].start()
        for k in range(depth):
            count_ref[k] = 0
        for i in range(ranks):
            copies[i].wait()
            for shard in range(shards):
                for tile in range(wide // TILE):
                    k = shard * (wide // TILE) + tile

                    @pl.when(row_flag_ref[tile_ref[r * ranks + i], k] != 0)
                    def _():
                        count = count_ref[k]
                        row_ref[k * ranks + count] = i
                        count_ref[k] = count + 1
                        rows = pl.ds(pl.multiple_of(count * TILE_ROWS, TILE_ROWS), TILE_ROWS)
                        value = tiles_ref[i, shard, :, pl.ds(tile * TILE, TILE)]
                        high = value.astype(jnp.bfloat16)
                        twice_ref[rows, pl.ds(2 * k * TILE, TILE)] = high
                        twice_ref[rows, pl.ds((2 * k + 1) * TILE, TILE)] = high
                        low_ref[rows, pl.ds(k * TILE, TILE)] = (value - high.astype(jnp.float32)).astype(
                            jnp.bfloat16
                        )

    total_ref[...] = jnp.zeros_like(total_ref)

    @pl.loop(0, depth)
    def _(k):
        needed = flag_ref[k, (first + step) * width // TILE] != 0
        here = pl.ds(pl.multiple_of(k * TILE, TILE), TILE)
        top = pl.ds(pl.multiple_of(2 * k * TILE, TILE), TILE)
        deep = pl.ds(pl.multiple_of(2 * k * TILE, TILE), 2 * TILE)
        for count in range(1, ranks + 1):

            @pl.when(jnp.logical_and(needed, count_ref[k] == count))
            def _():
                rows = pl.ds(0, count * TILE_ROWS)
                part = jnp.dot(low_ref[rows, here], halves_ref[top, :], preferred_element_type=jnp.float32)
                part = part + jnp.dot(
                    twice_ref[rows, deep], halves_ref[deep, :], preferred_element_type=jnp.float32
                )
                for j in range(count):
                    at = pl.ds(pl.multiple_of(row_ref[k * ranks + j] * TILE_ROWS, TILE_ROWS), TILE_ROWS)
                    total_ref[at, :] += part[j * TILE_ROWS : (j + 1) * TILE_ROWS]

    share = width // CHAINS
    for chain, (kept, sent) in enumerate(RANKS):
        columns = pl.ds(chain * share, share)
        for ref, peers in ((out_refs[2 * chain], kept), (out_refs[2 * chain + 1], sent)):
            for i, peer in enumerate(peers):
                ref[i] = total_ref[pl.ds(peer * TILE_ROWS, TILE_ROWS), columns]


def product(r, first, steps, ranks, source, tile, row_flags, int_tiles, gathered, halves):
    depth, width = halves.shape[0] // 2, halves.shape[1]
    shards = depth // gathered.shape[2]
    rows = ranks * TILE_ROWS
    share = COLUMNS // CHAINS

    integral = pl.BlockSpec((2 * depth, COLUMNS), lambda i, *_: (0, first + i))
    return pl.pallas_call(
        functools.partial(product_kernel, r, first, ranks),
        out_shape=[jax.ShapeDtypeStruct((2, TILE_ROWS, share * steps), jnp.float32)] * (2 * CHAINS),
        grid_spec=pltpu.PrefetchScalarGridSpec(
            num_scalar_prefetch=4,
            grid=(steps,),
            in_specs=[pl.BlockSpec(memory_space=pl.ANY), integral],
            out_specs=[pl.BlockSpec((2, TILE_ROWS, share), lambda i, *_: (0, 0, i))] * (2 * CHAINS),
            scratch_shapes=[
                pltpu.VMEM((ranks, shards, TILE_ROWS, depth // shards), jnp.float32),
                pltpu.VMEM((rows, 2 * depth), jnp.bfloat16),
                pltpu.VMEM((rows, depth), jnp.bfloat16),
                pltpu.VMEM((rows, COLUMNS), jnp.float32),
                pltpu.SMEM((depth // TILE,), jnp.int32),
                pltpu.SMEM((depth // TILE * ranks,), jnp.int32),
                pltpu.SemaphoreType.DMA((ranks,)),
            ],
        ),
        compiler_params=pltpu.CompilerParams(vmem_limit_bytes=VMEM_BYTES),
        cost_estimate=pl.CostEstimate(
            flops=6 * rows * depth * steps * COLUMNS, bytes_accessed=4 * depth * steps * COLUMNS, transcendentals=0
        ),
    )(source, tile, row_flags, int_tiles, gathered, halves)


def relay_kernel(*refs):
    for chain in range(CHAINS):
        refs[2 * CHAINS + chain][...] = refs[2 * chain][0] + refs[2 * chain + 1][0]


def relay(kept, heard):
    _, rows, width = kept[0].shape
    passed = pl.BlockSpec((1, rows, width), lambda i: (1, 0, 0))
    out = jax.ShapeDtypeStruct((rows, width), jnp.float32)
    return pl.pallas_call(
        relay_kernel,
        out_shape=[out] * CHAINS,
        grid=(1,),
        in_specs=[passed] * (2 * CHAINS),
        out_specs=[pl.BlockSpec((rows, width), lambda i: (0, 0))] * CHAINS,
    )(*[array for pair in zip(kept, heard) for array in pair])


def finish_kernel(columns, *refs):
    refs = refs[1:]
    parts, (term_ref, denominator_ref), out_ref = refs[: 3 * CHAINS], refs[3 * CHAINS : 3 * CHAINS + 2], refs[-1]
    share = columns // CHAINS
    for block in range(term_ref.shape[1] // columns):
        for chain in range(CHAINS):
            kept, heard, relayed = parts[3 * chain : 3 * chain + 3]
            source = pl.ds(block * share, share)
            target = pl.ds(block * columns + chain * share, share)
            total = kept[0, :, source] + heard[0, :, source] + relayed[:, source]
            out_ref[:, target] = (total + term_ref[:, target]) / denominator_ref[:, target]


def finish(r, start, slot, kept, heard, relayed, other_terms, denominators, update):
    blocks = 2 if start == 0 else 1
    share = kept[0].shape[2] // blocks
    width = share * CHAINS
    first = pl.BlockSpec((1, TILE_ROWS, share), lambda i, slot: (0, 0, i))
    whole = pl.BlockSpec((TILE_ROWS, share), lambda i, slot: (0, i))
    owned = pl.BlockSpec((TILE_ROWS, width), lambda i, slot: (slot[r], start * COLUMNS // width + i))
    before = [] if update is None else [update]
    return pl.pallas_call(
        functools.partial(finish_kernel, COLUMNS),
        out_shape=jax.ShapeDtypeStruct(other_terms.shape, jnp.float32),
        grid_spec=pltpu.PrefetchScalarGridSpec(
            num_scalar_prefetch=1,
            grid=(blocks,),
            in_specs=[first, first, whole] * CHAINS
            + [owned, owned]
            + [pl.BlockSpec(memory_space=pl.ANY)] * len(before),
            out_specs=owned,
        ),
        input_output_aliases={3 * CHAINS + 3: 0} if before else {},
        cost_estimate=pl.CostEstimate(flops=0, bytes_accessed=24 * TILE_ROWS * width, transcendentals=0),
    )(
        slot,
        *[array for chain in zip(kept, heard, relayed) for array in chain],
        other_terms,
        denominators,
        *before,
    )


def in_rounds(devices, ranks, amplitudes, amp_tiles, integrals, int_tiles, owner_tiles, other_terms, denominators):
    rank = lax.axis_index("cd").astype(jnp.int32)
    spot = lax.axis_index("ab").astype(jnp.int32)
    tiles = amp_tiles.shape[1]
    half = tiles // CORES

    def gather(array):
        return lax.all_gather(array, "ab", axis=0)

    def swap(sent, peers):
        return [lax.ppermute(array, "cd", [(c, c ^ peer) for c in range(ranks)]) for array, peer in zip(sent, peers)]

    where, source, slot, tile = plan(owner_tiles, jnp.stack([rank, spot]), devices, half)
    whole = take(FIRST, tiles, where, amp_tiles, amplitudes)
    halves = split(integrals)
    away = take(AWAY, half, where, amp_tiles, amplitudes)
    stay = take(STAY, half, where, amp_tiles, amplitudes)
    came = lax.ppermute(away, "ab", [(i, i ^ 1) for i in range(devices)])
    mine = where[WHOSE] == 0
    shards = [whole, jnp.where(mine, stay, came), jnp.where(mine, came, stay)]
    gathered = [gather(shard) for shard in shards]
    terms = (other_terms, denominators)
    tie = lax.optimization_barrier
    steps = halves.shape[1] // COLUMNS
    most = steps * 3 // 4

    def begin(r, rows, first=0, count=steps):
        return product(r, first, count, ranks, source, tile, row_flags, int_tiles, rows, halves)

    def send(parts):
        return swap(parts[1::2], (1, 2))

    def pass_on(parts, heard):
        onward = relay(parts[0::2], heard)
        return onward, swap(onward, (2, 1))

    row_flags, halves = tie((amp_tiles, halves))
    for bit in range((devices - 1).bit_length()):
        reach = 1 << bit
        came = lax.ppermute(row_flags, "ab", [(i, i ^ reach) for i in range(devices)])
        row_flags = jnp.where(
            spot & reach == 0, jnp.concatenate([row_flags, came]), jnp.concatenate([came, row_flags])
        )
    rows, halves, row_flags, *_ = tie((gathered[0], halves, row_flags, *shards[1:]))
    parts0 = begin(0, rows)
    heard0 = send(parts0)
    parts1, heard0 = tie((begin(1, rows), heard0))
    heard1 = send(parts1)
    onward, relayed0 = pass_on(parts0, heard0)

    onward, relayed1 = pass_on(parts1, heard1)
    rows, onward = tie((gathered[1], onward))
    parts2, relayed0, relayed1 = tie((begin(2, rows), relayed0, relayed1))
    parts2, slot, onward = tie((parts2, slot, onward))
    heard2 = send(parts2)
    update = finish(0, 0, slot, parts0[0::2], heard0, relayed0, *terms, None)
    update = finish(1, 0, slot, parts1[0::2], heard1, relayed1, *terms, update)
    heard2, update = tie((heard2, update))
    onward, relayed2 = pass_on(parts2, heard2)

    rows, onward, update = tie((gathered[2], onward, update))
    parts3, relayed2 = tie((begin(3, rows, 0, most), relayed2))
    heard3 = send(parts3)
    parts4, heard3 = tie((begin(3, rows, most, steps - most), heard3))
    heard4 = send(parts4)
    onward, relayed3 = pass_on(parts3, heard3)
    onward, relayed4 = pass_on(parts4, heard4)
    slot, onward = tie((slot, onward))
    update = finish(2, 0, slot, parts2[0::2], heard2, relayed2, *terms, update)
    update = finish(3, 0, slot, parts3[0::2], heard3, relayed3, *terms, update)
    return finish(3, most, slot, parts4[0::2], heard4, relayed4, *terms, update)


def solution(mesh):
    ranks, places = mesh.shape["cd"], mesh.shape["ab"]

    def on_device(amplitudes, amp_tiles, integrals, int_tiles, owner_tiles, other_terms, denominators):
        args = (amplitudes, amp_tiles, integrals, int_tiles, owner_tiles, other_terms, denominators)
        tiles = owner_tiles.shape[0]
        whole = places % CORES == 0 and amplitudes.shape[1] % (CORES * TILE) == 0
        if whole and ranks == 4 and tiles == 2 * places == ROUNDS * ranks:
            return in_rounds(places, ranks, *args)
        return plain(*args)

    return jax.shard_map(
        on_device,
        mesh=mesh,
        in_specs=(
            P("ab", "cd"),
            P("ab", "cd"),
            P("cd", "ab"),
            P("cd", "ab"),
            P(),
            P("cd", "ab"),
            P("cd", "ab"),
        ),
        out_specs=P("cd", "ab"),
        check_vma=False,
    )
```
